128 devices in a mesh: echo: 8 (over x, core), plane: 16 (over z, y).
Axes of the slice: x: 4, y: 4, z: 4, core: 2. Of those that a mesh axis runs over, the one named last changes fastest.
Arguments:
- acquired: bfloat16 [8, 8, 16, 256, 1024], P('echo', None, 'plane'), may hold values from -3 to 3
- coil_maps: bfloat16 [8, 16, 256, 1024], P(None, 'plane'), may hold values from -2.09375 to 2.09375
- mask_words: int32 [8, 256, 18], P('echo'), may hold values from 0 to 1073741823, as said below
- start_image: float32 [8, 16, 256, 1024], P('echo', 'plane'), may hold values from -36 to 36
Outputs:
- solved_image: float32 [8, 16, 256, 1024], P('echo', 'plane')
The draws below stay inside these ranges and needn't reach their ends.
Inputs may be any that keep to these rules, and one draw needn't show every extreme that they name: Bit j of mask_words[e, z, w] is 1 where echo e samples ky = 30 w + j at kz = z; bits for ky at or above 512 are 0.
All inputs are finite; a program needn't handle non-finite values.
Results may differ from the reference program's by a relative error of at most 0.0009.
Values sent between devices are 32-bit elements; how exact they have to be, the bound alone decides.
A program may use at most 192 MiB of HBM per device.

```python
import math
import jax
import jax.numpy as jnp
from jax import lax

NY = 512
NZ = 256
COILS = 8
ITERS = 2
ECHOES = 8
X = 16
WORDS = 18


def draw_mask_words(key, part):
    key = jax.random.fold_in(key, 29)
    draws = jax.random.randint(key, (ECHOES, NZ, WORDS, 30), 0, 3)
    bit = jnp.arange(30, dtype=jnp.int32)
    column = jnp.arange(WORDS, dtype=jnp.int32)[:, None] * 30 + bit[None, :]
    row = jnp.arange(NZ, dtype=jnp.int32)
    centre = ((row < 4) | (row >= NZ - 4))[:, None, None] & (column < 30)[None]
    taken = (draws == 0) | centre[None]
    taken = taken & (column < NY)[None, None]
    weights = jnp.left_shift(jnp.ones((30,), jnp.int32), bit)
    return jnp.sum(jnp.where(taken, weights, 0), axis=-1).astype(jnp.int32)


def draw_start_image(key, part):
    key = jax.random.fold_in(key, 17)
    base_key, scale_key = jax.random.split(key)
    shape = (ECHOES, X, NZ, 2 * NY)
    base = jnp.clip(jax.random.normal(base_key, shape, jnp.float32), -4.0, 4.0)
    spread = jnp.exp(jax.random.uniform(scale_key, (1, X, NZ, NY), jnp.float32, math.log(0.3), math.log(3.0)))
    spread = jnp.concatenate([spread, spread], -1)
    decay = 4.0 ** (-jnp.arange(ECHOES, dtype=jnp.float32) / max(ECHOES - 1, 1))
    profile = 1.0 + 2.0 * jnp.arange(X, dtype=jnp.float32) / max(X - 1, 1)
    return base * spread * decay[:, None, None, None] * profile[None, :, None, None]


def shard_levels(key, dims, cuts, low, top_value):
    factor_of = 1.0
    for position, shards_of in cuts:
        heights = jax.random.uniform(jax.random.fold_in(jax.random.fold_in(key, 6), position), (shards_of,), jnp.float32, low / len(cuts), top_value / len(cuts))
        factor_of = factor_of * jnp.repeat(jnp.exp(heights), dims[position] // shards_of).reshape((-1,) + (1,) * (len(dims) - 1 - position))
    return factor_of


def noise(rng, dims, deviation, most, pieces=(), held_as=jnp.bfloat16):
    factor_of = shard_levels(rng, dims, pieces, -0.22, 0.18) if pieces else 1.0
    values = jax.random.normal(rng, dims, jnp.float32) * deviation * factor_of
    return jnp.minimum(jnp.maximum(values, -most), most).astype(held_as)


def setup_inputs(seed: int = 0) -> dict:
    key_list = jax.random.split(jax.random.key(seed), 5)
    acquired = noise(key_list[0], (ECHOES, COILS, X, NZ, 2 * NY), 0.5, 3.0, ((0, 8), (2, 16)))
    coil_maps = noise(key_list[1], (COILS, X, NZ, 2 * NY), 0.35, 2.09375, ((1, 16),))
    mask_words = draw_mask_words(jax.random.fold_in(key_list[4], 71), 0)
    start_image = draw_start_image(jax.random.fold_in(key_list[4], 71), 0)
    return dict(acquired=acquired, coil_maps=coil_maps, mask_words=mask_words, start_image=start_image)


DUAL_STEP = 0.25
PRIMAL_STEP = 0.25
RADIUS_FACTOR = 0.5
EPSILON = 1e-06

def make_tables(count):
    index = jnp.arange(count, dtype=jnp.int32)
    angle = (index[:, None] * index[None, :] % count).astype(jnp.float32) * (2.0 * math.pi / count)
    scale = 1.0 / math.sqrt(count)
    return ((jnp.cos(angle) * scale).astype(jnp.bfloat16), (jnp.sin(angle) * scale).astype(jnp.bfloat16))

def ky_kernel(cosine, sine, forward):
    if forward:
        upper = jnp.concatenate([cosine, -sine], 1)
        lower = jnp.concatenate([sine, cosine], 1)
    else:
        upper = jnp.concatenate([cosine, sine], 1)
        lower = jnp.concatenate([-sine, cosine], 1)
    return jnp.concatenate([upper, lower], 0)

def along_kz(half, cosine, sine, forward, width):
    first = jnp.einsum('zw,bwk->bzk', cosine.astype(jnp.float32), half.astype(jnp.float32))
    second = jnp.einsum('zw,bwk->bzk', sine.astype(jnp.float32), half.astype(jnp.float32))
    if forward:
        real_part = first[..., :width] + second[..., width:]
        imaginary = first[..., width:] - second[..., :width]
    else:
        real_part = first[..., :width] - second[..., width:]
        imaginary = first[..., width:] + second[..., :width]
    return jnp.concatenate([real_part, imaginary], -1)

def times_maps(maps, field, width, conjugate):
    map_real = maps[..., :width].astype(jnp.float32)
    map_imaginary = maps[..., width:].astype(jnp.float32)
    field_real = field[..., :width]
    field_imaginary = field[..., width:]
    if conjugate:
        real_part = map_real * field_real + map_imaginary * field_imaginary
        imaginary = map_real * field_imaginary - map_imaginary * field_real
    else:
        real_part = map_real * field_real - map_imaginary * field_imaginary
        imaginary = map_real * field_imaginary + map_imaginary * field_real
    return jnp.concatenate([real_part, imaginary], -1)

def unpack_mask(words, width):
    spread = jnp.repeat(words, 30, axis=-1)[..., :width]
    offset = jnp.arange(width, dtype=jnp.int32) % 30
    sampled = (jnp.right_shift(spread, offset) % 2).astype(jnp.float32)
    return jnp.concatenate([sampled, sampled], -1)

def forward_model(image, maps, kernel, cosine, sine, width):
    coil = times_maps(maps[None], image[:, None], width, False).astype(jnp.bfloat16)
    shape = coil.shape
    half = jnp.dot(coil.reshape(-1, 2 * width), kernel, preferred_element_type=jnp.float32).astype(jnp.bfloat16)
    half = half.reshape(-1, shape[-2], 2 * width)
    return along_kz(half, cosine, sine, True, width).reshape(shape)

def adjoint_model(dual, maps, kernel, cosine, sine, width):
    shape = dual.shape
    flat = dual.astype(jnp.bfloat16).reshape(-1, shape[-2], 2 * width)
    half = along_kz(flat, cosine, sine, False, width).astype(jnp.bfloat16)
    spatial = jnp.dot(half.reshape(-1, 2 * width), kernel, preferred_element_type=jnp.float32).reshape(shape)
    return lax.optimization_barrier(jnp.sum(times_maps(maps[None], spatial, width, True), axis=1))

def inner_gradients(field, width):
    grad_z = jnp.concatenate([field[:, :, 1:] - field[:, :, :-1], jnp.zeros_like(field[:, :, :1])], 2)
    diff_y = jnp.concatenate([field[..., 1:] - field[..., :-1], jnp.zeros_like(field[..., :1])], 3)
    keep_y = jnp.arange(2 * width, dtype=jnp.int32) % width < width - 1
    return (grad_z, jnp.where(keep_y, diff_y, 0.0))

def inner_transpose(dual_z, dual_y):
    part_z = jnp.concatenate([jnp.zeros_like(dual_z[:, :, :1]), dual_z[:, :, :-1]], 2) - dual_z
    part_y = jnp.concatenate([jnp.zeros_like(dual_y[..., :1]), dual_y[..., :-1]], 3) - dual_y
    return part_z + part_y

def reference(acquired, coil_maps, mask_words, start_image):
    width = NY
    cos_y, sin_y = make_tables(NY)
    cos_z, sin_z = make_tables(NZ)
    kernel_forward = ky_kernel(cos_y, sin_y, True)
    kernel_inverse = ky_kernel(cos_y, sin_y, False)
    sampled = unpack_mask(mask_words, width)
    power = jnp.sum(start_image * start_image) / (ECHOES * X * NZ * NY)
    radius = RADIUS_FACTOR * jnp.sqrt(power + EPSILON)
    current = start_image
    extra = start_image
    dual_x = jnp.zeros_like(start_image)
    dual_z = jnp.zeros_like(start_image)
    dual_y = jnp.zeros_like(start_image)
    dual_data = jnp.zeros(acquired.shape, jnp.float32)
    for step in range(ITERS):
        grad_x = jnp.concatenate([extra[:, 1:] - extra[:, :-1], jnp.zeros_like(extra[:, :1])], 1)
        grad_z, grad_y = inner_gradients(extra, width)
        dual_x = dual_x + DUAL_STEP * grad_x
        dual_z = dual_z + DUAL_STEP * grad_z
        dual_y = dual_y + DUAL_STEP * grad_y
        squares = lax.optimization_barrier(jnp.sum(dual_x * dual_x + dual_z * dual_z + dual_y * dual_y, axis=0))
        squares = squares[..., :width] + squares[..., width:]
        shrink = 1.0 / jnp.maximum(1.0, jnp.sqrt(squares) / radius)
        shrink = jnp.concatenate([shrink, shrink], -1)[None]
        dual_x = dual_x * shrink
        dual_z = dual_z * shrink
        dual_y = dual_y * shrink

        def per_echo(items):
            image, data, mask, dual = items
            spectra = forward_model(image[None], coil_maps, kernel_forward, cos_z, sin_z, width)[0]
            dual = (dual + DUAL_STEP * mask[None, None] * (spectra - data.astype(jnp.float32))) / (1.0 + DUAL_STEP)
            back = adjoint_model(dual[None], coil_maps, kernel_inverse, cos_z, sin_z, width)[0]
            return (dual, back)
        dual_data, back = lax.map(per_echo, (extra, acquired, sampled, dual_data))
        part_x = jnp.concatenate([jnp.zeros_like(dual_x[:, :1]), dual_x[:, :-1]], 1) - dual_x
        transposed = part_x + inner_transpose(dual_z, dual_y)
        updated = current - PRIMAL_STEP * (back + transposed)
        extra = 2.0 * updated - current
        current = updated
    return current
```

```python
import functools
import math

import jax
import jax.numpy as jnp
import ml_dtypes
import numpy as np
from jax import lax
from jax.experimental import pallas as pl
from jax.experimental.pallas import tpu as pltpu
from jax.sharding import PartitionSpec as P

NY = 512
NZ = 256
COILS = 8
RADIUS_FACTOR = 0.5
EPSILON = 1e-06
ROWS = 16
CHUNKS = NZ // ROWS
JOBS = 2 * CHUNKS
MESH = pl.DeviceIdType.MESH
bf16 = jnp.bfloat16
f32 = jnp.float32

LAG_SEND = 3
START_PRIMAL = 16
START_SECOND = 28
START_COILS = 32
START_FINAL = 48
STEPS = START_FINAL + CHUNKS


def tables(count):
    index = np.arange(count, dtype=np.int64)
    angle = ((index[:, None] * index[None, :]) % count).astype(np.float32) * np.float32(
        2.0 * math.pi / count
    )
    scale = np.float32(1.0 / math.sqrt(count))
    return tuple(
        (part(angle).astype(np.float32) * scale).astype(ml_dtypes.bfloat16)
        for part in (np.cos, np.sin)
    )


def constants():
    cos_y, sin_y = tables(NY)
    cos_z, sin_z = tables(NZ)
    ky_forward, ky_inverse, kz_forward, kz_inverse = [], [], [], []
    for q in range(4):
        c, s = cos_y[:128, q::4], sin_y[:128, q::4]
        ky_forward.append(np.block([[c, -s], [s, c]]))
        ky_inverse.append(np.block([[c.T, s.T], [-s.T, c.T]]))
    for p in range(2):
        c, s = cos_z[p::2, :128], sin_z[p::2, :128]
        kz_forward.append(np.block([[c, s], [-s, c]]))
        kz_inverse.append(kz_forward[-1].T)
    rows = np.zeros((NZ, NZ), np.float32)
    for r in range(NZ):
        rows[r, (r % 128) * 2 + r // 128] = 1
    lanes = np.zeros((NY, NY), np.float32)
    for k in range(NY):
        lanes[k, (k % 4) * 128 + k // 4] = 1
    lane = np.arange(NY)
    ky = 4 * (lane % 128) + lane // 128
    where = np.zeros((8, NY), np.int32)
    where[0] = ky // 30
    where[1] = ky % 30
    cast = lambda a: np.ascontiguousarray(np.stack(a)).astype(ml_dtypes.bfloat16)
    return (
        cast(ky_forward),
        cast(ky_inverse),
        cast(kz_forward),
        cast(kz_inverse),
        rows.astype(ml_dtypes.bfloat16),
        lanes.astype(ml_dtypes.bfloat16),
        where,
    )


def dot(a, b):
    return jnp.dot(a, b, preferred_element_type=f32)


def permute_acquired(c, acq, acqp, rows, lanes, tmp):
    for n in range(4):
        sl = slice(n * 256, (n + 1) * 256)
        tmp[:, sl] = dot(rows[...], acq[c, :, sl]).astype(bf16)
    for part in range(2):
        for n in range(2):
            v = dot(
                tmp[:, part * 512 : (part + 1) * 512], lanes[:, n * 256 : (n + 1) * 256]
            ).astype(bf16)
            out = (slice(part * 128, (part + 1) * 128), slice(n * 256, (n + 1) * 256))
            acqp[(c, 0) + out] = v[:128]
            acqp[(c, 1) + out] = v[128:]


def coil_image(c, w, maps, xs):
    def body(b, _):
        r = pl.ds(pl.multiple_of(b * 16, 16), 16)
        xr, xi = [], []
        for t in range(4):
            l = slice(t * 128, (t + 1) * 128)
            h = slice(512 + t * 128, 512 + (t + 1) * 128)
            mr, mi = maps[c, r, l].astype(f32), maps[c, r, h].astype(f32)
            wr, wi = w[r, l], w[r, h]
            xr.append(mr * wr - mi * wi)
            xi.append(mr * wi + mi * wr)
        ar, ai, br, bi = xr[0] + xr[2], xi[0] + xi[2], xr[0] - xr[2], xi[0] - xi[2]
        cr, ci, dr, di = xr[1] + xr[3], xi[1] + xi[3], xr[1] - xr[3], xi[1] - xi[3]
        outs = [(ar + cr, ai + ci), (br + di, bi - dr), (ar - cr, ai - ci), (br - di, bi + dr)]
        for q, (re, im) in enumerate(outs):
            xs[r, q * 256 : q * 256 + 128] = re.astype(bf16)
            xs[r, q * 256 + 128 : q * 256 + 256] = im.astype(bf16)
        return 0

    lax.fori_loop(0, NZ // 16, body, 0, unroll=2)


def ky_forward(xs, kf, hs):
    for q in range(4):
        h = dot(xs[:, q * 256 : (q + 1) * 256], kf[q])
        s = (h[:128] + h[128:]).astype(bf16)
        d = (h[:128] - h[128:]).astype(bf16)
        l = slice(q * 128, (q + 1) * 128)
        hs[0, 0:128, l] = s[:, :128]
        hs[0, 128:256, l] = s[:, 128:]
        hs[1, 0:128, l] = d[:, :128]
        hs[1, 128:256, l] = d[:, 128:]


def kz_residual(c, hs, tf, acqp, mask, rs):
    for p in range(2):
        for n in range(2):
            l = slice(n * 256, (n + 1) * 256)
            y = dot(tf[p], hs[p, :, l])
            m = mask[p, :, l]
            for i in range(2):
                rr = slice(i * 128, (i + 1) * 128)
                rs[p, rr, l] = (y[rr] - acqp[c, p, rr, l].astype(f32)).astype(bf16) * m


def kz_inverse(rs, ti, hp):
    for n in range(2):
        l = slice(n * 256, (n + 1) * 256)
        e, o = dot(ti[0], rs[0, :, l]), dot(ti[1], rs[1, :, l])
        for first, v in ((0, (e + o).astype(bf16)), (128, (e - o).astype(bf16))):
            for k in range(2):
                base = (2 * n + k) * 256
                ll = slice(k * 128, (k + 1) * 128)
                hp[first : first + 128, base : base + 128] = v[:128, ll]
                hp[first : first + 128, base + 128 : base + 256] = v[128:, ll]


def ky_inverse(hp, ki, zs):
    for q in range(4):
        zs[:, q * 256 : (q + 1) * 256] = dot(hp[:, q * 256 : (q + 1) * 256], ki[q])


def coil_sum(c, zs, maps, d):
    def body(b, _):
        r = pl.ds(pl.multiple_of(b * 16, 16), 16)
        g = [(zs[r, q * 256 : q * 256 + 128], zs[r, q * 256 + 128 : q * 256 + 256]) for q in range(4)]
        ar, ai, br, bi = g[0][0] + g[2][0], g[0][1] + g[2][1], g[0][0] - g[2][0], g[0][1] - g[2][1]
        cr, ci, dr, di = g[1][0] + g[3][0], g[1][1] + g[3][1], g[1][0] - g[3][0], g[1][1] - g[3][1]
        z = [(ar + cr, ai + ci), (br - di, bi + dr), (ar - cr, ai - ci), (br + di, bi - dr)]
        for t in range(4):
            l = slice(t * 128, (t + 1) * 128)
            h = slice(512 + t * 128, 512 + (t + 1) * 128)
            mr, mi = maps[c, r, l].astype(f32), maps[c, r, h].astype(f32)
            zr, zi = z[t]
            d[r, l] += mr * zr + mi * zi
            d[r, h] += mr * zi - mi * zr
        return 0

    lax.fori_loop(0, NZ // 16, body, 0, unroll=2)


def build_mask(words, where, mask):
    column = where[0:1, :]
    bit = where[1:2, :]
    for p in range(2):
        for b in range(8):
            part = words[pl.ds(p + 32 * b, 16, stride=2), :]
            spread = jnp.zeros((16, NY), jnp.int32)
            for w in range(18):
                spread = jnp.where(column == w, part[:, w : w + 1], spread)
            value = jnp.right_shift(spread, jnp.broadcast_to(bit, (16, NY))) & 1
            mask[p, 16 * b : 16 * b + 16, :] = value.astype(f32).astype(bf16)


def kernel(
    acq_hbm, maps_hbm, words_hbm, u_hbm, kf_hbm, ki_hbm, tf_hbm, ti_hbm, rows_hbm, lanes_hbm, where_hbm,
    out_hbm,
    acq, maps, words, kf, ki, tf, ti, rows, lanes, where,
    acqp, mask, xs, hs, rs, hp, zs,
    cur, extra, w, d, px, pz, py, upb, pxprev,
    n2, crecv, half, xrecv, tot, pw, pw_recv, rad,
    in_sem, up_s, up_r, px_s, px_r, cs, cr, xsend, xrecv_sem, as_, ar, ps, pr, out_sem,
):
    e = lax.axis_index("echo")
    p = lax.axis_index("plane")
    core, x = lax.rem(e, 2), e // 2
    y, z = lax.rem(p, 4), p // 4
    has_up, has_down = p < 15, p > 0
    partner = (e + 1 - 2 * core, p)
    others_x = [(lax.rem(x + k, 4) * 2 + core, p) for k in (1, 2, 3)]
    others_y = [(e, z * 4 + lax.rem(y + k, 4)) for k in (1, 2, 3)]
    others_z = [(e, lax.rem(z + k, 4) * 4 + y) for k in (1, 2, 3)]
    up, down = (e, p + 1), (e, p - 1)

    barrier = pltpu.get_barrier_semaphore()
    greet = [partner] + others_x + others_y + others_z
    for device in greet:
        pl.semaphore_signal(barrier, inc=1, device_id=device, device_id_type=MESH)

    @pl.when(has_up)
    def _():
        pl.semaphore_signal(barrier, inc=1, device_id=up, device_id_type=MESH)

    @pl.when(has_down)
    def _():
        pl.semaphore_signal(barrier, inc=1, device_id=down, device_id_type=MESH)

    loads = [(u_hbm, cur), (words_hbm, words), (where_hbm, where), (rows_hbm, rows), (lanes_hbm, lanes)]
    loads += [(kf_hbm, kf), (tf_hbm, tf), (ti_hbm, ti), (ki_hbm, ki)]
    for c in range(COILS):
        loads += [(acq_hbm.at[c], acq.at[c]), (maps_hbm.at[c], maps.at[c])]
    copies = [pltpu.make_async_copy(a, b, in_sem.at[i]) for i, (a, b) in enumerate(loads)]
    for copy in copies:
        copy.start()

    px[...] = jnp.zeros_like(px)
    pz[...] = jnp.zeros_like(pz)
    py[...] = jnp.zeros_like(py)
    d[...] = jnp.zeros_like(d)
    extra[NZ : NZ + 8, :] = jnp.zeros((8, 2 * NY), f32)

    pl.semaphore_wait(barrier, len(greet) + has_up.astype(jnp.int32) + has_down.astype(jnp.int32))

    def span(c, offset=0):
        return pl.ds(pl.multiple_of(c * ROWS + offset, 8), ROWS)

    def send_up(j, source):
        it, c = j // CHUNKS, lax.rem(j, CHUNKS)
        return pltpu.make_async_remote_copy(
            src_ref=source.at[span(c)],
            dst_ref=upb.at[it, span(c)],
            send_sem=up_s.at[j],
            recv_sem=up_r.at[j],
            device_id=down,
            device_id_type=MESH,
        )

    def send_dual(j):
        it, c = j // CHUNKS, lax.rem(j, CHUNKS)
        return pltpu.make_async_remote_copy(
            src_ref=px.at[span(c)],
            dst_ref=pxprev.at[it, span(c)],
            send_sem=px_s.at[j],
            recv_sem=px_r.at[j],
            device_id=up,
            device_id_type=MESH,
        )

    mine = pl.ds(pl.multiple_of(core * 8, 8), 8)
    theirs = pl.ds(pl.multiple_of(8 - core * 8, 8), 8)

    def send_half(j):
        return pltpu.make_async_remote_copy(
            src_ref=n2.at[j, theirs],
            dst_ref=crecv.at[j],
            send_sem=cs.at[j],
            recv_sem=cr.at[j],
            device_id=partner,
            device_id_type=MESH,
        )

    def send_x(j, k):
        return pltpu.make_async_remote_copy(
            src_ref=half.at[j],
            dst_ref=xrecv.at[k, j],
            send_sem=xsend.at[k, j],
            recv_sem=xrecv_sem.at[k, j],
            device_id=others_x[k],
            device_id_type=MESH,
        )

    def send_total(j):
        return pltpu.make_async_remote_copy(
            src_ref=tot.at[j, mine],
            dst_ref=tot.at[j, mine],
            send_sem=as_.at[j],
            recv_sem=ar.at[j],
            device_id=partner,
            device_id_type=MESH,
        )

    power_groups = [[partner], others_x, others_y, others_z]
    power_first = [0, 1, 4, 7]

    def send_power(stage, k):
        slot = power_first[stage] + k
        return pltpu.make_async_remote_copy(
            src_ref=pw.at[stage],
            dst_ref=pw_recv.at[slot],
            send_sem=ps.at[slot],
            recv_sem=pr.at[slot],
            device_id=power_groups[stage][k],
            device_id_type=MESH,
        )

    @pl.when(has_down)
    def _():
        def body(j, _):
            send_up(j, u_hbm).start()
            return 0

        lax.fori_loop(0, CHUNKS, body, 0)

    copies[0].wait()

    def power_body(b, total):
        r = pl.ds(pl.multiple_of(b * 8, 8), 8)
        v = cur[r, :]
        extra[r, :] = v
        w[r, :] = v
        s = v * v
        for k in range(8):
            total = total + s[:, k * 128 : (k + 1) * 128]
        return total

    pw[0] = lax.fori_loop(0, NZ // 8, power_body, jnp.zeros((8, 128), f32), unroll=2)
    send_power(0, 0).start()
    for copy in copies[1:9]:
        copy.wait()
    build_mask(words, where, mask)

    lane = lax.broadcasted_iota(jnp.int32, (ROWS, 2 * NY), 1) & (NY - 1)
    row = lax.broadcasted_iota(jnp.int32, (ROWS, 2 * NY), 0)

    def squares(j):
        it, c = j // CHUNKS, lax.rem(j, CHUNKS)

        @pl.when(has_up)
        def _():
            send_up(j, extra).wait_recv()

            @pl.when(it == 1)
            def _():
                send_dual(j - CHUNKS).wait_send()

        r = span(c)
        wide = extra[pl.ds(pl.multiple_of(c * ROWS, 8), ROWS + 8), :]
        here = wide[:ROWS]
        gx = jnp.where(has_up, upb[it, r, :] - here, 0.0)
        gz = jnp.where(row + c * ROWS < NZ - 1, wide[1 : ROWS + 1] - here, 0.0)
        gy = jnp.where(lane < NY - 1, pltpu.roll(here, 2 * NY - 1, 1) - here, 0.0)
        rz = span(c, 8)
        vx = px[r, :] + 0.25 * gx
        vz = pz[rz, :] + 0.25 * gz
        vy = py[r, :] + 0.25 * gy
        px[r, :] = vx
        pz[rz, :] = vz
        py[r, :] = vy
        s = vx * vx + vz * vz + vy * vy
        n2[j] = s[:, :NY] + s[:, NY:]
        send_half(j).start()

    def halves(j):
        send_half(j).wait_recv()
        half[j] = n2[j, mine, :] + crecv[j]
        for k in range(3):
            send_x(j, k).start()

    def totals(j):
        for k in range(3):
            send_x(j, k).wait_recv()
        tot[j, mine, :] = (half[j] + xrecv[0, j]) + (xrecv[1, j] + xrecv[2, j])
        send_total(j).start()

    def shrink(j):
        c = lax.rem(j, CHUNKS)
        send_total(j).wait_recv()
        s = jnp.minimum(1.0, rad[0:1, 0:1] * lax.rsqrt(tot[j]))
        s = jnp.concatenate([s, s], 1)
        r, rz = span(c), span(c, 8)
        px[r, :] = px[r, :] * s
        pz[rz, :] = pz[rz, :] * s
        py[r, :] = py[r, :] * s

        @pl.when(has_up)
        def _():
            send_dual(j).start()

    def primal(j):
        it, c = j // CHUNKS, lax.rem(j, CHUNKS)

        @pl.when(has_down)
        def _():
            send_dual(j).wait_recv()

        r = span(c)
        below = jnp.where(has_down, pxprev[it, r, :], 0.0)
        wide = pz[pl.ds(pl.multiple_of(c * ROWS, 8), ROWS + 8), :]
        vy = py[r, :]
        before = jnp.where(lane > 0, pltpu.roll(vy, 1, 1), 0.0)
        g = (below - px[r, :]) + (wide[7 : ROWS + 7] - wide[8:]) + (before - vy)
        factor = jnp.where(it == 0, 0.2, 0.36).astype(f32)
        old = cur[r, :]
        new = old - 0.25 * (factor * d[r, :] + g)
        cur[r, :] = new

        @pl.when(it == 0)
        def _():
            ahead = 2.0 * new - old
            extra[r, :] = ahead
            w[r, :] = (0.2 / 0.36) * ahead + (0.16 / 0.36) * old
            d[r, :] = jnp.zeros((ROWS, 2 * NY), f32)

            @pl.when(has_down)
            def _():
                send_up(j + CHUNKS, extra).start()

        @pl.when(it == 1)
        def _():
            store(c).start()

    def store(c):
        return pltpu.make_async_copy(cur.at[span(c)], out_hbm.at[span(c)], out_sem.at[c])

    def coil_first(it, c):
        @pl.when(it == 0)
        def _():
            pltpu.make_async_copy(acq_hbm.at[c], acq.at[c], in_sem.at[9 + 2 * c]).wait()
            pltpu.make_async_copy(maps_hbm.at[c], maps.at[c], in_sem.at[10 + 2 * c]).wait()
            permute_acquired(c, acq, acqp, rows, lanes, xs)

        coil_image(c, w, maps, xs)
        ky_forward(xs, kf, hs)

    def coil_second(c):
        kz_residual(c, hs, tf, acqp, mask, rs)
        kz_inverse(rs, ti, hp)
        ky_inverse(hp, ki, zs)
        coil_sum(c, zs, maps, d)

    def step(t, _):
        for stage in range(4):

            @pl.when(t == stage)
            def _(stage=stage):
                total = pw[stage]
                for k in range(len(power_groups[stage])):
                    send_power(stage, k).wait_recv()
                    total = total + pw_recv[power_first[stage] + k]
                if stage < 3:
                    pw[stage + 1] = total
                    for k in range(3):
                        send_power(stage + 1, k).start()
                else:
                    mean = jnp.sum(total) * (1.0 / 16777216.0) + EPSILON
                    rad[...] = RADIUS_FACTOR * jnp.sqrt(jnp.broadcast_to(mean, (8, 128)))

        first = t - START_SECOND + CHUNKS

        def job(lag):
            a, b = t - lag, first - lag
            valid_a = (a >= 0) & (a < CHUNKS)
            valid_b = (b >= CHUNKS) & (b < JOBS)
            return valid_a | valid_b, jnp.where(valid_a, a, b)

        def run(lag, work):
            valid, j = job(lag)

            @pl.when(valid)
            def _():
                work(j)

        run(2, totals)
        run(0, squares)
        second = t >= START_COILS
        it = second.astype(jnp.int32)
        part = t - jnp.where(second, START_COILS, 0)

        @pl.when((part < 2 * COILS) & (lax.rem(part, 2) == 0))
        def _():
            coil_first(it, part // 2)

        @pl.when((part < 2 * COILS) & (lax.rem(part, 2) == 1))
        def _():
            coil_second(part // 2)

        run(0, halves)
        run(LAG_SEND, shrink)

        a, b = t - START_PRIMAL, t - START_FINAL
        valid_a = (a >= 0) & (a < CHUNKS)

        @pl.when(valid_a | (b >= 0))
        def _():
            primal(jnp.where(valid_a, a, b + CHUNKS))

        return 0

    lax.fori_loop(0, STEPS, step, 0)

    for stage in range(4):
        for k in range(len(power_groups[stage])):
            send_power(stage, k).wait_send()

    def drain(j, _):
        send_half(j).wait_send()
        for k in range(3):
            send_x(j, k).wait_send()
        send_total(j).wait_send()

        @pl.when(has_down)
        def _():
            send_up(j, extra).wait_send()

        @pl.when(has_up & (j >= CHUNKS))
        def _():
            send_dual(j).wait_send()

        @pl.when(j < CHUNKS)
        def _():
            store(j).wait()

        return 0

    lax.fori_loop(0, JOBS, drain, 0)


def shards(acquired, coil_maps, mask_words, start_image):
    acquired = acquired.reshape(COILS, NZ, 2 * NY)
    coil_maps = coil_maps.reshape(COILS, NZ, 2 * NY)
    words = mask_words.reshape(NZ, 18)
    image = start_image.reshape(NZ, 2 * NY)
    consts = [jnp.asarray(a) for a in constants()]
    anywhere = pl.BlockSpec(memory_space=pl.ANY)
    vmem = lambda shape, dtype=f32: pltpu.VMEM(shape, dtype)
    dma = lambda *shape: pltpu.SemaphoreType.DMA(shape)
    scratch = [
        vmem((COILS, NZ, 2 * NY), bf16),
        vmem((COILS, NZ, 2 * NY), bf16),
        vmem((NZ, 18), jnp.int32),
        vmem((4, 256, 256), bf16),
        vmem((4, 256, 256), bf16),
        vmem((2, 256, 256), bf16),
        vmem((2, 256, 256), bf16),
        vmem((256, 256), bf16),
        vmem((512, 512), bf16),
        vmem((8, NY), jnp.int32),
        vmem((COILS, 2, 256, 512), bf16),
        vmem((2, 128, 512), bf16),
        vmem((256, 1024), bf16),
        vmem((2, 256, 512), bf16),
        vmem((2, 256, 512), bf16),
        vmem((256, 1024), bf16),
        vmem((256, 1024)),
        vmem((NZ, 2 * NY)),
        vmem((NZ + 8, 2 * NY)),
        vmem((NZ, 2 * NY)),
        vmem((NZ, 2 * NY)),
        vmem((NZ, 2 * NY)),
        vmem((NZ + 8, 2 * NY)),
        vmem((NZ, 2 * NY)),
        vmem((2, NZ, 2 * NY)),
        vmem((2, NZ, 2 * NY)),
        vmem((JOBS, ROWS, NY)),
        vmem((JOBS, 8, NY)),
        vmem((JOBS, 8, NY)),
        vmem((3, JOBS, 8, NY)),
        vmem((JOBS, ROWS, NY)),
        vmem((4, 8, 128)),
        vmem((10, 8, 128)),
        vmem((8, 128)),
        dma(9 + 2 * COILS),
        dma(JOBS),
        dma(JOBS),
        dma(JOBS),
        dma(JOBS),
        dma(JOBS),
        dma(JOBS),
        dma(3, JOBS),
        dma(3, JOBS),
        dma(JOBS),
        dma(JOBS),
        dma(10),
        dma(10),
        dma(CHUNKS),
    ]
    solved = pl.pallas_call(
        kernel,
        out_shape=jax.ShapeDtypeStruct((NZ, 2 * NY), f32),
        in_specs=[anywhere] * 11,
        out_specs=anywhere,
        scratch_shapes=scratch,
        compiler_params=pltpu.CompilerParams(
            collective_id=0, has_side_effects=True, vmem_limit_bytes=60 * 2**20
        ),
        name="solve",
    )(acquired, coil_maps, words, image, *consts)
    return solved.reshape(start_image.shape)


def solution(mesh):
    in_specs = (
        P("echo", None, "plane", None, None),
        P(None, "plane", None, None),
        P("echo", None, None),
        P("echo", "plane", None, None),
    )
    out_specs = P("echo", "plane", None, None)
    return jax.shard_map(shards, mesh=mesh, in_specs=in_specs, out_specs=out_specs, check_vma=False)
```

```python
import functools
import math

import jax
import jax.numpy as jnp
import ml_dtypes
import numpy as np
from jax import lax
from jax.experimental import pallas as pl
from jax.experimental.pallas import tpu as pltpu
from jax.sharding import PartitionSpec as P

NY = 512
NZ = 256
COILS = 8
RADIUS_FACTOR = 0.5
EPSILON = 1e-06
ROWS = 16
CHUNKS = NZ // ROWS
JOBS = 2 * CHUNKS
MESH = pl.DeviceIdType.MESH
bf16 = jnp.bfloat16
f32 = jnp.float32

HALF = ROWS // 2

AHEAD = 3
ORDER = ("pow", "us", "sh", "to", "ha", "sq", "coil", "pr")
STEPS = 96
PLANS = {
    "pow": 0xA0,
    "us": 0x196B6D,
    "to": 0x2CDA64D46C2982278B000,
    "ha": 0x15CA8CD23980561B2D80,
    "sh": 0x43339932AB14C08B94A000,
    "pr": 0xFFFF000025629927A0000000,
    "sq": 0x3B2934A95300C5A7360,
    "coil": 0xF5D540000000244A55BF,
}


SEGMENT = 24


def plan_word(stage, segment):
    plan = PLANS[stage]
    word = jnp.int32(0)
    for i in range(-(-STEPS // SEGMENT)):
        bits = jnp.int32((plan >> (SEGMENT * i)) & (2**SEGMENT - 1))
        word = jnp.where(segment == i, bits, word)
    return word


def tables(count):
    index = np.arange(count, dtype=np.int64)
    angle = ((index[:, None] * index[None, :]) % count).astype(np.float32) * np.float32(
        2.0 * math.pi / count
    )
    scale = np.float32(1.0 / math.sqrt(count))
    return tuple(
        (part(angle).astype(np.float32) * scale).astype(ml_dtypes.bfloat16)
        for part in (np.cos, np.sin)
    )


def constants():
    cos_y, sin_y = tables(NY)
    cos_z, sin_z = tables(NZ)
    ky_forward, ky_inverse, kz_forward, kz_inverse = [], [], [], []
    for q in range(4):
        c, s = cos_y[:128, q::4], sin_y[:128, q::4]
        ky_forward.append(np.block([[c, -s], [s, c]]))
        ky_inverse.append(np.block([[c.T, s.T], [-s.T, c.T]]))
    for p in range(2):
        c, s = cos_z[p::2, :128], sin_z[p::2, :128]
        kz_forward.append(np.block([[c, s], [-s, c]]))
        kz_inverse.append(kz_forward[-1].T)
    rows = np.zeros((NZ, NZ), np.float32)
    for r in range(NZ):
        rows[r, (r % 128) * 2 + r // 128] = 1
    lanes = np.zeros((NY, NY), np.float32)
    for k in range(NY):
        lanes[k, (k % 4) * 128 + k // 4] = 1
    lane = np.arange(NY)
    ky = 4 * (lane % 128) + lane // 128
    bits = np.zeros((8, NY), np.int32)
    bits[0] = ky % 30 % 8
    spread = np.zeros((128, NY), np.float32)
    spread[ky % 30 // 8 * 32 + ky // 30, lane] = 1
    cast = lambda a: np.ascontiguousarray(np.stack(a)).astype(ml_dtypes.bfloat16)
    return (
        cast(ky_forward),
        cast(ky_inverse),
        cast(kz_forward),
        cast(kz_inverse),
        rows.astype(ml_dtypes.bfloat16),
        lanes.astype(ml_dtypes.bfloat16),
        spread.astype(ml_dtypes.bfloat16),
        bits,
    )


def dot(a, b):
    return jnp.dot(a, b, preferred_element_type=f32)


def permute_acquired(c, acq, acqp, rows, lanes, tmp):
    for n in range(4):
        sl = slice(n * 256, (n + 1) * 256)
        tmp[:, sl] = dot(rows[...], acq[c, :, sl]).astype(bf16)
    for part in range(2):
        for n in range(2):
            v = dot(
                tmp[:, part * 512 : (part + 1) * 512], lanes[:, n * 256 : (n + 1) * 256]
            ).astype(bf16)
            out = (slice(part * 128, (part + 1) * 128), slice(n * 256, (n + 1) * 256))
            acqp[(c, 0) + out] = v[:128]
            acqp[(c, 1) + out] = v[128:]


def coil_image(c, w, maps, xs):
    for b in range(NZ // 16):
        r = slice(b * 16, b * 16 + 16)
        xr, xi = [], []
        for t in range(4):
            l = slice(t * 128, (t + 1) * 128)
            h = slice(512 + t * 128, 512 + (t + 1) * 128)
            mr, mi = maps[c, r, l].astype(f32), maps[c, r, h].astype(f32)
            wr, wi = w[r, l], w[r, h]
            xr.append(mr * wr - mi * wi)
            xi.append(mr * wi + mi * wr)
        ar, ai, br, bi = xr[0] + xr[2], xi[0] + xi[2], xr[0] - xr[2], xi[0] - xi[2]
        cr, ci, dr, di = xr[1] + xr[3], xi[1] + xi[3], xr[1] - xr[3], xi[1] - xi[3]
        outs = [(ar + cr, ai + ci), (br + di, bi - dr), (ar - cr, ai - ci), (br - di, bi + dr)]
        for q, (re, im) in enumerate(outs):
            xs[r, q * 256 : q * 256 + 128] = re.astype(bf16)
            xs[r, q * 256 + 128 : q * 256 + 256] = im.astype(bf16)


def ky_forward(xs, kf, hs):
    for q in range(4):
        h = dot(xs[:, q * 256 : (q + 1) * 256], kf[q])
        s = (h[:128] + h[128:]).astype(bf16)
        d = (h[:128] - h[128:]).astype(bf16)
        l = slice(q * 128, (q + 1) * 128)
        hs[0, 0:128, l] = s[:, :128]
        hs[0, 128:256, l] = s[:, 128:]
        hs[1, 0:128, l] = d[:, :128]
        hs[1, 128:256, l] = d[:, 128:]


def kz_residual(c, hs, tf, acqp, mask, rs):
    for p in range(2):
        for n in range(2):
            l = slice(n * 256, (n + 1) * 256)
            y = dot(tf[p], hs[p, :, l])
            m = mask[p, :, l]
            for i in range(2):
                rr = slice(i * 128, (i + 1) * 128)
                rs[p, rr, l] = (y[rr] - acqp[c, p, rr, l].astype(f32)).astype(bf16) * m


def kz_inverse(rs, ti, hp):
    for n in range(2):
        l = slice(n * 256, (n + 1) * 256)
        e, o = dot(ti[0], rs[0, :, l]), dot(ti[1], rs[1, :, l])
        for first, v in ((0, (e + o).astype(bf16)), (128, (e - o).astype(bf16))):
            for k in range(2):
                base = (2 * n + k) * 256
                ll = slice(k * 128, (k + 1) * 128)
                hp[first : first + 128, base : base + 128] = v[:128, ll]
                hp[first : first + 128, base + 128 : base + 256] = v[128:, ll]


def ky_inverse(hp, ki, zs):
    for q in range(4):
        zs[:, q * 256 : (q + 1) * 256] = dot(hp[:, q * 256 : (q + 1) * 256], ki[q])


def coil_sum(coils, zs, maps, d):
    for b in range(NZ // 16):
        r = slice(b * 16, b * 16 + 16)
        sums = [None] * 8
        for i, c in enumerate(coils):
            g = [(zs[i, r, q * 256 : q * 256 + 128], zs[i, r, q * 256 + 128 : q * 256 + 256]) for q in range(4)]
            ar, ai, br, bi = g[0][0] + g[2][0], g[0][1] + g[2][1], g[0][0] - g[2][0], g[0][1] - g[2][1]
            cr, ci, dr, di = g[1][0] + g[3][0], g[1][1] + g[3][1], g[1][0] - g[3][0], g[1][1] - g[3][1]
            z = [(ar + cr, ai + ci), (br - di, bi + dr), (ar - cr, ai - ci), (br + di, bi - dr)]
            for t in range(4):
                l = slice(t * 128, (t + 1) * 128)
                h = slice(512 + t * 128, 512 + (t + 1) * 128)
                mr, mi = maps[c, r, l].astype(f32), maps[c, r, h].astype(f32)
                zr, zi = z[t]
                re, im = mr * zr + mi * zi, mr * zi - mi * zr
                sums[t] = re if i == 0 else sums[t] + re
                sums[4 + t] = im if i == 0 else sums[4 + t] + im
        for t in range(8):
            d[r, t * 128 : (t + 1) * 128] += sums[t]


def build_mask(words, turned, spread, bits, mask):
    wide = jnp.concatenate([words[...].reshape(18, NZ), jnp.zeros((14, NZ), jnp.int32)], 0)
    turned[...] = jnp.concatenate([jnp.right_shift(wide, 8 * k) & 255 for k in range(4)], 0).T
    for p in range(2):
        byte = turned[pl.ds(p, 128, stride=2), :].astype(f32).astype(bf16)
        for n in range(2):
            l = slice(n * 256, (n + 1) * 256)
            value = dot(byte, spread[:, l]).astype(jnp.int32)
            bit = jnp.right_shift(value, jnp.broadcast_to(bits[0:1, l], (128, 256))) & 1
            mask[p, :, l] = bit.astype(f32).astype(bf16)


def kernel(
    acq_hbm, maps_hbm, words_hbm, u_hbm, kf_hbm, ki_hbm, tf_hbm, ti_hbm, rows_hbm, lanes_hbm, spread_hbm, bits_hbm,
    out_hbm,
    acq, maps, words, turned, kf, ki, tf, ti, rows, lanes, spread, bits,
    acqp, mask, xs, hs, rs, hp, zs,
    cur, extra, w, d, px, pz, py, upb, pxprev,
    n2, crecv, half, xrecv, tot, pw, pw_recv, rad,
    in_sem, up_s, up_r, px_s, px_r, cs, cr, xsend, xrecv_sem, as_, ar, ps, pr, out_sem,
):
    e = lax.axis_index("echo")
    p = lax.axis_index("plane")
    core, x = lax.rem(e, 2), e // 2
    y, z = lax.rem(p, 4), p // 4
    has_up, has_down = p < 15, p > 0
    partner = (e + 1 - 2 * core, p)
    others_x = [(lax.rem(x + k, 4) * 2 + core, p) for k in (1, 2, 3)]
    others_plane = [
        (e, lax.rem(z + b, 4) * 4 + lax.rem(y + a, 4)) for a in range(4) for b in range(4) if a or b
    ]
    up, down = (e, p + 1), (e, p - 1)

    barrier = pltpu.get_barrier_semaphore()
    greet = [partner] + others_x + others_plane
    for device in greet:
        pl.semaphore_signal(barrier, inc=1, device_id=device, device_id_type=MESH)

    @pl.when(has_up)
    def _():
        pl.semaphore_signal(barrier, inc=1, device_id=up, device_id_type=MESH)

    @pl.when(has_down)
    def _():
        pl.semaphore_signal(barrier, inc=1, device_id=down, device_id_type=MESH)

    loads = [(u_hbm, cur), (words_hbm, words), (spread_hbm, spread), (bits_hbm, bits), (rows_hbm, rows), (lanes_hbm, lanes)]
    loads += [(kf_hbm, kf), (tf_hbm, tf), (ti_hbm, ti), (ki_hbm, ki)]
    for c in range(COILS):
        loads += [(acq_hbm.at[c], acq.at[c]), (maps_hbm.at[c], maps.at[c])]
    copies = [pltpu.make_async_copy(a, b, in_sem.at[i]) for i, (a, b) in enumerate(loads)]
    for copy in copies:
        copy.start()

    px[...] = jnp.zeros_like(px)
    pz[...] = jnp.zeros_like(pz)
    py[...] = jnp.zeros_like(py)
    d[...] = jnp.zeros_like(d)
    extra[NZ : NZ + 8, :] = jnp.zeros((8, 2 * NY), f32)

    copies[0].wait()

    def power_body(b, total):
        r = pl.ds(pl.multiple_of(b * 8, 8), 8)
        v = cur[r, :]
        extra[r, :] = v
        w[r, :] = v
        s = v * v
        for k in range(8):
            total = total + s[:, k * 128 : (k + 1) * 128]
        return total

    pw[0] = lax.fori_loop(0, NZ // 8, power_body, jnp.zeros((8, 128), f32), unroll=2)
    pl.semaphore_wait(barrier, len(greet) + has_up.astype(jnp.int32) + has_down.astype(jnp.int32))

    def span(c, offset=0):
        return pl.ds(pl.multiple_of(c * ROWS + offset, 8), ROWS)

    def send_up(j, source):
        it, c = j // CHUNKS, lax.rem(j, CHUNKS)
        return pltpu.make_async_remote_copy(
            src_ref=source.at[span(c)],
            dst_ref=upb.at[it, span(c)],
            send_sem=up_s.at[j],
            recv_sem=up_r.at[j],
            device_id=down,
            device_id_type=MESH,
        )

    def send_dual(j):
        it, c = j // CHUNKS, lax.rem(j, CHUNKS)
        return pltpu.make_async_remote_copy(
            src_ref=px.at[span(c)],
            dst_ref=pxprev.at[it, span(c)],
            send_sem=px_s.at[j],
            recv_sem=px_r.at[j],
            device_id=up,
            device_id_type=MESH,
        )

    mine = pl.ds(pl.multiple_of(core * HALF, 8), HALF)
    theirs = pl.ds(pl.multiple_of(HALF - core * HALF, 8), HALF)

    def send_half(j):
        return pltpu.make_async_remote_copy(
            src_ref=n2.at[j, theirs],
            dst_ref=crecv.at[j],
            send_sem=cs.at[j],
            recv_sem=cr.at[j],
            device_id=partner,
            device_id_type=MESH,
        )

    def send_x(j, k):
        return pltpu.make_async_remote_copy(
            src_ref=half.at[j],
            dst_ref=xrecv.at[k, j],
            send_sem=xsend.at[k, j],
            recv_sem=xrecv_sem.at[k, j],
            device_id=others_x[k],
            device_id_type=MESH,
        )

    def send_total(j):
        return pltpu.make_async_remote_copy(
            src_ref=tot.at[j, mine],
            dst_ref=tot.at[j, mine],
            send_sem=as_.at[j],
            recv_sem=ar.at[j],
            device_id=partner,
            device_id_type=MESH,
        )

    power_groups = [others_plane, others_x, [partner]]
    power_first = [0, 15, 18]

    def send_power(stage, k):
        slot = power_first[stage] + k
        return pltpu.make_async_remote_copy(
            src_ref=pw.at[stage],
            dst_ref=pw_recv.at[slot],
            send_sem=ps.at[slot],
            recv_sem=pr.at[slot],
            device_id=power_groups[stage][k],
            device_id_type=MESH,
        )

    for k in range(15):
        send_power(0, k).start()
    for copy in copies[1:10]:
        copy.wait()
    build_mask(words, turned, spread, bits, mask)

    lane = lax.broadcasted_iota(jnp.int32, (ROWS, 2 * NY), 1) & (NY - 1)
    row = lax.broadcasted_iota(jnp.int32, (ROWS, 2 * NY), 0)

    def squares(j):
        it, c = j // CHUNKS, lax.rem(j, CHUNKS)

        @pl.when(has_up)
        def _():
            send_up(j, extra).wait_recv()

            @pl.when(it == 1)
            def _():
                send_dual(j - CHUNKS).wait_send()

        r = span(c)
        wide = extra[pl.ds(pl.multiple_of(c * ROWS, 8), ROWS + 8), :]
        here = wide[:ROWS]
        gx = jnp.where(has_up, upb[it, r, :] - here, 0.0)
        gz = jnp.where(row + c * ROWS < NZ - 1, wide[1 : ROWS + 1] - here, 0.0)
        gy = jnp.where(lane < NY - 1, pltpu.roll(here, 2 * NY - 1, 1) - here, 0.0)
        rz = span(c, 8)
        vx = px[r, :] + 0.25 * gx
        vz = pz[rz, :] + 0.25 * gz
        vy = py[r, :] + 0.25 * gy
        px[r, :] = vx
        pz[rz, :] = vz
        py[r, :] = vy
        s = vx * vx + vz * vz + vy * vy
        n2[j] = s[:, :NY] + s[:, NY:]
        send_half(j).start()

    def halves(j):
        send_half(j).wait_recv()
        half[j] = n2[j, mine, :] + crecv[j]
        for k in range(3):
            send_x(j, k).start()

    def totals(j):
        for k in range(3):
            send_x(j, k).wait_recv()
        tot[j, mine, :] = (half[j] + xrecv[0, j]) + (xrecv[1, j] + xrecv[2, j])
        send_total(j).start()

    def shrink(j):
        c = lax.rem(j, CHUNKS)
        send_total(j).wait_recv()
        s = jnp.minimum(1.0, rad[0:1, 0:1] * lax.rsqrt(tot[j]))
        s = jnp.concatenate([s, s], 1)
        r, rz = span(c), span(c, 8)
        px[r, :] = px[r, :] * s
        pz[rz, :] = pz[rz, :] * s
        py[r, :] = py[r, :] * s

        @pl.when(has_up)
        def _():
            send_dual(j).start()

    def primal(j):
        it, c = j // CHUNKS, lax.rem(j, CHUNKS)

        @pl.when(has_down)
        def _():
            send_dual(j).wait_recv()

        send_half(j).wait_send()
        for k in range(3):
            send_x(j, k).wait_send()
        send_total(j).wait_send()

        @pl.when(has_down)
        def _():
            send_up(j, cur).wait_send()

        r = span(c)
        below = jnp.where(has_down, pxprev[it, r, :], 0.0)
        wide = pz[pl.ds(pl.multiple_of(c * ROWS, 8), ROWS + 8), :]
        vy = py[r, :]
        before = jnp.where(lane > 0, pltpu.roll(vy, 1, 1), 0.0)
        g = (below - px[r, :]) + (wide[7 : ROWS + 7] - wide[8:]) + (before - vy)
        factor = jnp.where(it == 0, 0.2, 0.36).astype(f32)
        old = cur[r, :]
        new = old - 0.25 * (factor * d[r, :] + g)
        cur[r, :] = new

        @pl.when(it == 0)
        def _():
            ahead = 2.0 * new - old
            extra[r, :] = ahead
            w[r, :] = (0.2 / 0.36) * ahead + (0.16 / 0.36) * old
            d[r, :] = jnp.zeros((ROWS, 2 * NY), f32)

            @pl.when(has_down)
            def _():
                send_up(j + CHUNKS, extra).start()

        @pl.when(it == 1)
        def _():
            store(c).start()

    def store(c):
        return pltpu.make_async_copy(cur.at[span(c)], out_hbm.at[span(c)], out_sem.at[c])

    def coil_permute(c):
        for i in range(2):
            at = 10 + 2 * (c + i)
            pltpu.make_async_copy(acq_hbm.at[c + i], acq.at[c + i], in_sem.at[at]).wait()
            pltpu.make_async_copy(maps_hbm.at[c + i], maps.at[c + i], in_sem.at[at + 1]).wait()
        for i in range(2):
            permute_acquired(c + i, acq, acqp, rows, lanes, xs.at[i])

    def coil_first(c):
        for i in range(2):
            coil_image(c + i, w, maps, xs.at[i])
        for i in range(2):
            ky_forward(xs.at[i], kf, hs.at[i])

    def coil_second(c):
        for i in range(2):
            kz_residual(c + i, hs.at[i], tf, acqp, mask, rs.at[i])
        for i in range(2):
            kz_inverse(rs.at[i], ti, hp.at[i])

    def coil_third(c):
        for i in range(2):
            ky_inverse(hp.at[i], ki, zs.at[i])
        coil_sum([c, c + 1], zs, maps, d)

    def power(stage_now):
        for stage in range(3):

            @pl.when(jnp.int32(stage_now) == stage)
            def _(stage=stage):
                total = pw[stage]
                for k in range(len(power_groups[stage])):
                    send_power(stage, k).wait_recv()
                    total = total + pw_recv[power_first[stage] + k]
                if stage < 2:
                    pw[stage + 1] = total
                    for k in range(len(power_groups[stage + 1])):
                        send_power(stage + 1, k).start()
                else:
                    mean = jnp.sum(total) * (1.0 / 16777216.0) + EPSILON
                    rad[...] = RADIUS_FACTOR * jnp.sqrt(jnp.broadcast_to(mean, (8, 128)))

    def start_up(j):
        @pl.when(has_down)
        def _():
            send_up(j + AHEAD, cur).start()

    def coil_work(i):
        early = i < 16
        s = i - 16
        c = 2 * jnp.where(early, i // 4, s // 3)
        part = jnp.where(early, lax.rem(i, 4), lax.rem(s, 3) + 1)
        for k, work in enumerate((coil_permute, coil_first, coil_second, coil_third)):

            @pl.when(part == k)
            def _(work=work):
                work(c)

    works = dict(
        pow=power, us=start_up, sq=squares, ha=halves, to=totals, sh=shrink, pr=primal, coil=coil_work
    )

    def segment(n, done):
        words = [plan_word(stage, n) for stage in ORDER]

        def step(t, done):
            after = []
            for stage, word, count in zip(ORDER, words, done):
                now = jnp.right_shift(word, t) & 1

                @pl.when(now == 1)
                def _(stage=stage, count=count):
                    works[stage](count)

                after.append(count + now)
            return tuple(after)

        return lax.fori_loop(0, SEGMENT, step, done)

    power(0)

    @pl.when(has_down)
    def _():
        for j in range(AHEAD):
            send_up(j, cur).start()

    done = tuple(jnp.int32(int(stage == "pow")) for stage in ORDER)
    lax.fori_loop(0, -(-STEPS // SEGMENT), segment, done)

    for stage in range(3):
        for k in range(len(power_groups[stage])):
            send_power(stage, k).wait_send()

    def drain(c, _):
        store(c).wait()

        @pl.when(has_up)
        def _():
            send_dual(c + CHUNKS).wait_send()

        return 0

    lax.fori_loop(0, CHUNKS, drain, 0)


def shards(acquired, coil_maps, mask_words, start_image):
    acquired = acquired.reshape(COILS, NZ, 2 * NY)
    coil_maps = coil_maps.reshape(COILS, NZ, 2 * NY)
    words = jnp.transpose(mask_words, (2, 0, 1))
    image = start_image.reshape(NZ, 2 * NY)
    consts = [jnp.asarray(a) for a in constants()]
    anywhere = pl.BlockSpec(memory_space=pl.ANY)
    vmem = lambda shape, dtype=f32: pltpu.VMEM(shape, dtype)
    dma = lambda *shape: pltpu.SemaphoreType.DMA(shape)
    scratch = [
        vmem((COILS, NZ, 2 * NY), bf16),
        vmem((COILS, NZ, 2 * NY), bf16),
        vmem((18, 1, NZ), jnp.int32),
        vmem((NZ, 128), jnp.int32),
        vmem((4, 256, 256), bf16),
        vmem((4, 256, 256), bf16),
        vmem((2, 256, 256), bf16),
        vmem((2, 256, 256), bf16),
        vmem((256, 256), bf16),
        vmem((512, 512), bf16),
        vmem((128, NY), bf16),
        vmem((8, NY), jnp.int32),
        vmem((COILS, 2, 256, 512), bf16),
        vmem((2, 128, 512), bf16),
        vmem((2, 256, 1024), bf16),
        vmem((2, 2, 256, 512), bf16),
        vmem((2, 2, 256, 512), bf16),
        vmem((2, 256, 1024), bf16),
        vmem((2, 256, 1024)),
        vmem((NZ, 2 * NY)),
        vmem((NZ + 8, 2 * NY)),
        vmem((NZ, 2 * NY)),
        vmem((NZ, 2 * NY)),
        vmem((NZ, 2 * NY)),
        vmem((NZ + 8, 2 * NY)),
        vmem((NZ, 2 * NY)),
        vmem((2, NZ, 2 * NY)),
        vmem((2, NZ, 2 * NY)),
        vmem((JOBS, ROWS, NY)),
        vmem((JOBS, HALF, NY)),
        vmem((JOBS, HALF, NY)),
        vmem((3, JOBS, HALF, NY)),
        vmem((JOBS, ROWS, NY)),
        vmem((3, 8, 128)),
        vmem((19, 8, 128)),
        vmem((8, 128)),
        dma(10 + 2 * COILS),
        dma(JOBS),
        dma(JOBS),
        dma(JOBS),
        dma(JOBS),
        dma(JOBS),
        dma(JOBS),
        dma(3, JOBS),
        dma(3, JOBS),
        dma(JOBS),
        dma(JOBS),
        dma(19),
        dma(19),
        dma(CHUNKS),
    ]
    solved = pl.pallas_call(
        kernel,
        out_shape=jax.ShapeDtypeStruct((NZ, 2 * NY), f32),
        in_specs=[anywhere] * 12,
        out_specs=anywhere,
        scratch_shapes=scratch,
        compiler_params=pltpu.CompilerParams(
            collective_id=0, has_side_effects=True, vmem_limit_bytes=60 * 2**20
        ),
        name="solve",
    )(acquired, coil_maps, words, image, *consts)
    return solved.reshape(start_image.shape)


def solution(mesh):
    in_specs = (
        P("echo", None, "plane", None, None),
        P(None, "plane", None, None),
        P("echo", None, None),
        P("echo", "plane", None, None),
    )
    out_specs = P("echo", "plane", None, None)
    return jax.shard_map(shards, mesh=mesh, in_specs=in_specs, out_specs=out_specs, check_vma=False)
```

```python
import functools
import math

import jax
import jax.numpy as jnp
import ml_dtypes
import numpy as np
from jax import lax
from jax.experimental import pallas as pl
from jax.experimental.pallas import tpu as pltpu
from jax.sharding import PartitionSpec as P

NY = 512
NZ = 256
COILS = 8
RADIUS_FACTOR = 0.5
EPSILON = 1e-06
ROWS = 32
CHUNKS = NZ // ROWS
JOBS = 2 * CHUNKS
MESH = pl.DeviceIdType.MESH
bf16 = jnp.bfloat16
f32 = jnp.float32

HALF = ROWS // 2

BEFORE = 1
AHEAD = 2
ORDER = ("pow", "us", "sq", "to", "pr", "ha", "coil", "sh", "fin")
STEPS = 50
PLANS = {
    "pow": 0x60,
    "us": 0xA53,
    "to": 0x2A8B9E91040,
    "ha": 0x2A5CE92504,
    "sh": 0x4A93AF24080,
    "pr": 0x384AA3AF00000,
    "sq": 0x153AE24A42,
    "coil": 0x3FF600D9FFE,
    "fin": 0x3FC0000000000,
}


SEGMENT = 24


def plan_word(stage, segment):
    plan = PLANS[stage]
    word = jnp.int32(0)
    for i in range(-(-STEPS // SEGMENT)):
        bits = jnp.int32((plan >> (SEGMENT * i)) & (2**SEGMENT - 1))
        word = jnp.where(segment == i, bits, word)
    return word


def tables(count):
    index = np.arange(count, dtype=np.int64)
    angle = ((index[:, None] * index[None, :]) % count).astype(np.float32) * np.float32(
        2.0 * math.pi / count
    )
    scale = np.float32(1.0 / math.sqrt(count))
    return tuple(
        (part(angle).astype(np.float32) * scale).astype(ml_dtypes.bfloat16)
        for part in (np.cos, np.sin)
    )


def constants():
    cos_y, sin_y = tables(NY)
    cos_z, sin_z = tables(NZ)
    ky_forward, ky_inverse, kz_forward, kz_inverse = [], [], [], []
    for q in range(4):
        c, s = cos_y[:128, q::4], sin_y[:128, q::4]
        ky_forward.append(np.block([[c, -s], [s, c]]))
        ky_inverse.append(np.block([[c.T, s.T], [-s.T, c.T]]))
    for p in range(2):
        c, s = cos_z[p::2, :128], sin_z[p::2, :128]
        kz_forward.append(np.block([[c, s], [-s, c]]))
        kz_inverse.append(kz_forward[-1].T)
    rows = np.zeros((NZ, NZ), np.float32)
    for r in range(NZ):
        rows[r, (r % 128) * 2 + r // 128] = 1
    lanes = np.zeros((NY, NY), np.float32)
    for k in range(NY):
        lanes[k, (k % 4) * 128 + k // 4] = 1
    lane = np.arange(NY)
    ky = 4 * (lane % 128) + lane // 128
    bits = np.zeros((8, NY), np.int32)
    bits[0] = ky % 30 % 8
    spread = np.zeros((128, NY), np.float32)
    spread[ky % 30 // 8 * 32 + ky // 30, lane] = 1
    cast = lambda a: np.ascontiguousarray(np.stack(a)).astype(ml_dtypes.bfloat16)
    return (
        cast(ky_forward),
        cast(ky_inverse),
        cast(kz_forward),
        cast(kz_inverse),
        rows.astype(ml_dtypes.bfloat16),
        lanes.astype(ml_dtypes.bfloat16),
        spread.astype(ml_dtypes.bfloat16),
        bits,
    )


def dot(a, b):
    return jnp.dot(a, b, preferred_element_type=f32)


def permute_acquired(c, acq, acqp, rows, lanes, tmp):
    for n in range(4):
        sl = slice(n * 256, (n + 1) * 256)
        tmp[:, sl] = dot(rows[...], acq[c, :, sl]).astype(bf16)
    for part in range(2):
        for n in range(2):
            v = dot(
                tmp[:, part * 512 : (part + 1) * 512], lanes[:, n * 256 : (n + 1) * 256]
            ).astype(bf16)
            out = (slice(part * 128, (part + 1) * 128), slice(n * 256, (n + 1) * 256))
            acqp[(c, 0) + out] = v[:128]
            acqp[(c, 1) + out] = v[128:]


def coil_image(c, w, maps, xs):
    for b in range(NZ // 16):
        r = slice(b * 16, b * 16 + 16)
        xr, xi = [], []
        for t in range(4):
            l = slice(t * 128, (t + 1) * 128)
            h = slice(512 + t * 128, 512 + (t + 1) * 128)
            mr, mi = maps[c, r, l].astype(f32), maps[c, r, h].astype(f32)
            wr, wi = w[r, l], w[r, h]
            xr.append(mr * wr - mi * wi)
            xi.append(mr * wi + mi * wr)
        ar, ai, br, bi = xr[0] + xr[2], xi[0] + xi[2], xr[0] - xr[2], xi[0] - xi[2]
        cr, ci, dr, di = xr[1] + xr[3], xi[1] + xi[3], xr[1] - xr[3], xi[1] - xi[3]
        outs = [(ar + cr, ai + ci), (br + di, bi - dr), (ar - cr, ai - ci), (br - di, bi + dr)]
        for q, (re, im) in enumerate(outs):
            xs[r, q * 256 : q * 256 + 128] = re.astype(bf16)
            xs[r, q * 256 + 128 : q * 256 + 256] = im.astype(bf16)


def ky_forward(xs, kf, hs):
    for q in range(4):
        h = dot(xs[:, q * 256 : (q + 1) * 256], kf[q])
        s = (h[:128] + h[128:]).astype(bf16)
        d = (h[:128] - h[128:]).astype(bf16)
        l = slice(q * 128, (q + 1) * 128)
        hs[0, 0:128, l] = s[:, :128]
        hs[0, 128:256, l] = s[:, 128:]
        hs[1, 0:128, l] = d[:, :128]
        hs[1, 128:256, l] = d[:, 128:]


def kz_residual(c, hs, tf, acqp, mask, rs):
    for p in range(2):
        for n in range(2):
            l = slice(n * 256, (n + 1) * 256)
            y = dot(tf[p], hs[p, :, l])
            m = mask[p, :, l]
            for i in range(2):
                rr = slice(i * 128, (i + 1) * 128)
                rs[p, rr, l] = (y[rr] - acqp[c, p, rr, l].astype(f32)).astype(bf16) * m


def kz_inverse(rs, ti, hp):
    for n in range(2):
        l = slice(n * 256, (n + 1) * 256)
        e, o = dot(ti[0], rs[0, :, l]), dot(ti[1], rs[1, :, l])
        for first, v in ((0, (e + o).astype(bf16)), (128, (e - o).astype(bf16))):
            for k in range(2):
                base = (2 * n + k) * 256
                ll = slice(k * 128, (k + 1) * 128)
                hp[first : first + 128, base : base + 128] = v[:128, ll]
                hp[first : first + 128, base + 128 : base + 256] = v[128:, ll]


def ky_inverse(hp, ki, zs):
    for q in range(4):
        zs[:, q * 256 : (q + 1) * 256] = dot(hp[:, q * 256 : (q + 1) * 256], ki[q])


def coil_sum(coils, zs, maps, d):
    for b in range(NZ // 16):
        r = slice(b * 16, b * 16 + 16)
        sums = [None] * 8
        for i, c in enumerate(coils):
            g = [(zs[i, r, q * 256 : q * 256 + 128], zs[i, r, q * 256 + 128 : q * 256 + 256]) for q in range(4)]
            ar, ai, br, bi = g[0][0] + g[2][0], g[0][1] + g[2][1], g[0][0] - g[2][0], g[0][1] - g[2][1]
            cr, ci, dr, di = g[1][0] + g[3][0], g[1][1] + g[3][1], g[1][0] - g[3][0], g[1][1] - g[3][1]
            z = [(ar + cr, ai + ci), (br - di, bi + dr), (ar - cr, ai - ci), (br + di, bi - dr)]
            for t in range(4):
                l = slice(t * 128, (t + 1) * 128)
                h = slice(512 + t * 128, 512 + (t + 1) * 128)
                mr, mi = maps[c, r, l].astype(f32), maps[c, r, h].astype(f32)
                zr, zi = z[t]
                re, im = mr * zr + mi * zi, mr * zi - mi * zr
                sums[t] = re if i == 0 else sums[t] + re
                sums[4 + t] = im if i == 0 else sums[4 + t] + im
        for t in range(8):
            d[r, t * 128 : (t + 1) * 128] += sums[t]


def build_mask(words, turned, spread, bits, mask):
    wide = jnp.concatenate([words[...].reshape(18, NZ), jnp.zeros((14, NZ), jnp.int32)], 0)
    turned[...] = jnp.concatenate([jnp.right_shift(wide, 8 * k) & 255 for k in range(4)], 0).T
    for p in range(2):
        byte = turned[pl.ds(p, 128, stride=2), :].astype(f32).astype(bf16)
        for n in range(2):
            l = slice(n * 256, (n + 1) * 256)
            value = dot(byte, spread[:, l]).astype(jnp.int32)
            bit = jnp.right_shift(value, jnp.broadcast_to(bits[0:1, l], (128, 256))) & 1
            mask[p, :, l] = bit.astype(f32).astype(bf16)


def kernel(
    acq_hbm, maps_hbm, words_hbm, u_hbm, kf_hbm, ki_hbm, tf_hbm, ti_hbm, rows_hbm, lanes_hbm, spread_hbm, bits_hbm,
    out_hbm,
    acq, maps, words, turned, kf, ki, tf, ti, rows, lanes, spread, bits,
    acqp, mask, xs, hs, rs, hp, zs,
    cur, extra, w, d, px, pz, py, upb, pxprev,
    n2, crecv, half, xrecv, tot, pw, pw_recv, rad,
    in_sem, up_s, up_r, px_s, px_r, cs, cr, xsend, xrecv_sem, as_, ar, ps, pr, out_sem,
):
    e = lax.axis_index("echo")
    p = lax.axis_index("plane")
    core, x = lax.rem(e, 2), e // 2
    y, z = lax.rem(p, 4), p // 4
    has_up, has_down = p < 15, p > 0
    partner = (e + 1 - 2 * core, p)
    others_x = [(lax.rem(x + k, 4) * 2 + core, p) for k in (1, 2, 3)]
    others_plane = [
        (e, lax.rem(z + b, 4) * 4 + lax.rem(y + a, 4)) for a in range(4) for b in range(4) if a or b
    ]
    up, down = (e, p + 1), (e, p - 1)

    barrier = pltpu.get_barrier_semaphore()
    greet = [partner] + others_x + others_plane
    for device in greet:
        pl.semaphore_signal(barrier, inc=1, device_id=device, device_id_type=MESH)

    @pl.when(has_up)
    def _():
        pl.semaphore_signal(barrier, inc=1, device_id=up, device_id_type=MESH)

    @pl.when(has_down)
    def _():
        pl.semaphore_signal(barrier, inc=1, device_id=down, device_id_type=MESH)

    loads = [(u_hbm, cur), (words_hbm, words), (spread_hbm, spread), (bits_hbm, bits), (rows_hbm, rows), (lanes_hbm, lanes)]
    loads += [(kf_hbm, kf), (tf_hbm, tf), (ti_hbm, ti), (ki_hbm, ki)]
    for c in range(COILS):
        loads += [(acq_hbm.at[c], acq.at[c]), (maps_hbm.at[c], maps.at[c])]
    copies = [pltpu.make_async_copy(a, b, in_sem.at[i]) for i, (a, b) in enumerate(loads)]
    for copy in copies:
        copy.start()

    px[...] = jnp.zeros_like(px)
    pz[...] = jnp.zeros_like(pz)
    py[...] = jnp.zeros_like(py)
    d[...] = jnp.zeros_like(d)
    extra[NZ : NZ + 8, :] = jnp.zeros((8, 2 * NY), f32)

    copies[0].wait()

    def power_body(b, total):
        r = pl.ds(pl.multiple_of(b * 8, 8), 8)
        v = cur[r, :]
        extra[r, :] = v
        w[r, :] = v
        s = v * v
        for k in range(8):
            total = total + s[:, k * 128 : (k + 1) * 128]
        return total

    pw[0] = lax.fori_loop(0, NZ // 8, power_body, jnp.zeros((8, 128), f32), unroll=2)
    pl.semaphore_wait(barrier, len(greet) + has_up.astype(jnp.int32) + has_down.astype(jnp.int32))

    def span(c, offset=0):
        return pl.ds(pl.multiple_of(c * ROWS + offset, 8), ROWS)

    def send_up(j, source):
        it, c = j // CHUNKS, lax.rem(j, CHUNKS)
        return pltpu.make_async_remote_copy(
            src_ref=source.at[span(c)],
            dst_ref=upb.at[it, span(c)],
            send_sem=up_s.at[j],
            recv_sem=up_r.at[j],
            device_id=down,
            device_id_type=MESH,
        )

    def send_dual(j):
        it, c = j // CHUNKS, lax.rem(j, CHUNKS)
        return pltpu.make_async_remote_copy(
            src_ref=px.at[span(c)],
            dst_ref=pxprev.at[it, span(c)],
            send_sem=px_s.at[j],
            recv_sem=px_r.at[j],
            device_id=up,
            device_id_type=MESH,
        )

    mine = pl.ds(pl.multiple_of(core * HALF, 8), HALF)
    theirs = pl.ds(pl.multiple_of(HALF - core * HALF, 8), HALF)

    def send_half(j):
        return pltpu.make_async_remote_copy(
            src_ref=n2.at[j, theirs],
            dst_ref=crecv.at[j],
            send_sem=cs.at[j],
            recv_sem=cr.at[j],
            device_id=partner,
            device_id_type=MESH,
        )

    def send_x(j, k):
        return pltpu.make_async_remote_copy(
            src_ref=half.at[j],
            dst_ref=xrecv.at[k, j],
            send_sem=xsend.at[k, j],
            recv_sem=xrecv_sem.at[k, j],
            device_id=others_x[k],
            device_id_type=MESH,
        )

    def send_total(j):
        return pltpu.make_async_remote_copy(
            src_ref=tot.at[j, mine],
            dst_ref=tot.at[j, mine],
            send_sem=as_.at[j],
            recv_sem=ar.at[j],
            device_id=partner,
            device_id_type=MESH,
        )

    power_groups = [others_plane, others_x, [partner]]
    power_first = [0, 15, 18]

    def send_power(stage, k):
        slot = power_first[stage] + k
        return pltpu.make_async_remote_copy(
            src_ref=pw.at[stage],
            dst_ref=pw_recv.at[slot],
            send_sem=ps.at[slot],
            recv_sem=pr.at[slot],
            device_id=power_groups[stage][k],
            device_id_type=MESH,
        )

    for k in range(15):
        send_power(0, k).start()
    @pl.when(has_down)
    def _():
        for j in range(BEFORE):
            send_up(j, cur).start()

    for copy in copies[1:10]:
        copy.wait()
    build_mask(words, turned, spread, bits, mask)

    lane = lax.broadcasted_iota(jnp.int32, (ROWS, 2 * NY), 1) & (NY - 1)
    row = lax.broadcasted_iota(jnp.int32, (ROWS, 2 * NY), 0)

    def squares(j):
        it, c = j // CHUNKS, lax.rem(j, CHUNKS)

        @pl.when(has_up)
        def _():
            send_up(j, extra).wait_recv()

            @pl.when(it == 1)
            def _():
                send_dual(j - CHUNKS).wait_send()

        r = span(c)
        wide = extra[pl.ds(pl.multiple_of(c * ROWS, 8), ROWS + 8), :]
        here = wide[:ROWS]
        gx = jnp.where(has_up, upb[it, r, :] - here, 0.0)
        gz = jnp.where(row + c * ROWS < NZ - 1, wide[1 : ROWS + 1] - here, 0.0)
        gy = jnp.where(lane < NY - 1, pltpu.roll(here, 2 * NY - 1, 1) - here, 0.0)
        rz = span(c, 8)
        vx = px[r, :] + 0.25 * gx
        vz = pz[rz, :] + 0.25 * gz
        vy = py[r, :] + 0.25 * gy
        px[r, :] = vx
        pz[rz, :] = vz
        py[r, :] = vy
        s = vx * vx + vz * vz + vy * vy
        n2[j] = s[:, :NY] + s[:, NY:]
        send_half(j).start()

    def halves(j):
        send_half(j).wait_recv()
        half[j] = n2[j, mine, :] + crecv[j]
        for k in range(3):
            send_x(j, k).start()

    def totals(j):
        for k in range(3):
            send_x(j, k).wait_recv()
        tot[j, mine, :] = (half[j] + xrecv[0, j]) + (xrecv[1, j] + xrecv[2, j])
        send_total(j).start()

    def shrink(j):
        c = lax.rem(j, CHUNKS)
        send_total(j).wait_recv()
        s = jnp.minimum(1.0, rad[0:1, 0:1] * lax.rsqrt(tot[j]))
        s = jnp.concatenate([s, s], 1)
        r, rz = span(c), span(c, 8)
        px[r, :] = px[r, :] * s
        pz[rz, :] = pz[rz, :] * s
        py[r, :] = py[r, :] * s

        @pl.when(has_up)
        def _():
            send_dual(j).start()

    def primal(j):
        it, c = j // CHUNKS, lax.rem(j, CHUNKS)

        @pl.when(has_down)
        def _():
            send_dual(j).wait_recv()

        send_half(j).wait_send()
        for k in range(3):
            send_x(j, k).wait_send()
        send_total(j).wait_send()

        @pl.when(has_down)
        def _():
            send_up(j, cur).wait_send()

        r = span(c)
        below = jnp.where(has_down, pxprev[it, r, :], 0.0)
        wide = pz[pl.ds(pl.multiple_of(c * ROWS, 8), ROWS + 8), :]
        vy = py[r, :]
        before = jnp.where(lane > 0, pltpu.roll(vy, 1, 1), 0.0)
        g = (below - px[r, :]) + (wide[7 : ROWS + 7] - wide[8:]) + (before - vy)
        old = cur[r, :]
        new = old - 0.25 * g

        @pl.when(it == 0)
        def _():
            first = new - 0.05 * d[r, :]
            ahead = 2.0 * first - old
            cur[r, :] = first
            extra[r, :] = ahead
            w[r, :] = (0.2 / 0.36) * ahead + (0.16 / 0.36) * old
            d[r, :] = jnp.zeros((ROWS, 2 * NY), f32)

            @pl.when(has_down)
            def _():
                send_up(j + CHUNKS, extra).start()

        @pl.when(it == 1)
        def _():
            cur[r, :] = new

    def finish(c):
        r = span(c)
        cur[r, :] = cur[r, :] - 0.09 * d[r, :]
        store(c).start()

    def store(c):
        return pltpu.make_async_copy(cur.at[span(c)], out_hbm.at[span(c)], out_sem.at[c])

    def coil_permute(c):
        for i in range(2):
            at = 10 + 2 * (c + i)
            pltpu.make_async_copy(acq_hbm.at[c + i], acq.at[c + i], in_sem.at[at]).wait()
            pltpu.make_async_copy(maps_hbm.at[c + i], maps.at[c + i], in_sem.at[at + 1]).wait()
        for i in range(2):
            permute_acquired(c + i, acq, acqp, rows, lanes, xs.at[i])

    def coil_first(c):
        for i in range(2):
            coil_image(c + i, w, maps, xs.at[i])
        for i in range(2):
            ky_forward(xs.at[i], kf, hs.at[i])

    def coil_second(c):
        for i in range(2):
            kz_residual(c + i, hs.at[i], tf, acqp, mask, rs.at[i])
        for i in range(2):
            kz_inverse(rs.at[i], ti, hp.at[i])

    def coil_third(c):
        for i in range(2):
            ky_inverse(hp.at[i], ki, zs.at[i])
        coil_sum([c, c + 1], zs, maps, d)

    def power(stage_now):
        for stage in range(3):

            @pl.when(jnp.int32(stage_now) == stage)
            def _(stage=stage):
                total = pw[stage]
                for k in range(len(power_groups[stage])):
                    send_power(stage, k).wait_recv()
                    total = total + pw_recv[power_first[stage] + k]
                if stage < 2:
                    pw[stage + 1] = total
                    for k in range(len(power_groups[stage + 1])):
                        send_power(stage + 1, k).start()
                else:
                    mean = jnp.sum(total) * (1.0 / 16777216.0) + EPSILON
                    rad[...] = RADIUS_FACTOR * jnp.sqrt(jnp.broadcast_to(mean, (8, 128)))

    def start_up(j):
        @pl.when(has_down)
        def _():
            send_up(j + AHEAD, cur).start()

    def coil_work(i):
        early = i < 16
        s = i - 16
        c = 2 * jnp.where(early, i // 4, s // 3)
        part = jnp.where(early, lax.rem(i, 4), lax.rem(s, 3) + 1)
        for k, work in enumerate((coil_permute, coil_first, coil_second, coil_third)):

            @pl.when(part == k)
            def _(work=work):
                work(c)

    works = dict(
        pow=power, us=start_up, sq=squares, ha=halves, to=totals, sh=shrink, pr=primal, fin=finish, coil=coil_work
    )

    def segment(n, done):
        words = [plan_word(stage, n) for stage in ORDER]

        def step(t, done):
            after = []
            for stage, word, count in zip(ORDER, words, done):
                now = jnp.right_shift(word, t) & 1

                @pl.when(now == 1)
                def _(stage=stage, count=count):
                    works[stage](count)

                after.append(count + now)
            return tuple(after)

        return lax.fori_loop(0, SEGMENT, step, done)

    power(0)

    @pl.when(has_down)
    def _():
        for j in range(BEFORE, AHEAD):
            send_up(j, cur).start()

    done = tuple(jnp.int32(int(stage == "pow")) for stage in ORDER)
    lax.fori_loop(0, -(-STEPS // SEGMENT), segment, done)

    for stage in range(3):
        for k in range(len(power_groups[stage])):
            send_power(stage, k).wait_send()

    def drain(c, _):
        store(c).wait()

        @pl.when(has_up)
        def _():
            send_dual(c + CHUNKS).wait_send()

        return 0

    lax.fori_loop(0, CHUNKS, drain, 0)


def shards(acquired, coil_maps, mask_words, start_image):
    acquired = acquired.reshape(COILS, NZ, 2 * NY)
    coil_maps = coil_maps.reshape(COILS, NZ, 2 * NY)
    words = jnp.transpose(mask_words, (2, 0, 1))
    image = start_image.reshape(NZ, 2 * NY)
    consts = [jnp.asarray(a) for a in constants()]
    anywhere = pl.BlockSpec(memory_space=pl.ANY)
    vmem = lambda shape, dtype=f32: pltpu.VMEM(shape, dtype)
    dma = lambda *shape: pltpu.SemaphoreType.DMA(shape)
    scratch = [
        vmem((COILS, NZ, 2 * NY), bf16),
        vmem((COILS, NZ, 2 * NY), bf16),
        vmem((18, 1, NZ), jnp.int32),
        vmem((NZ, 128), jnp.int32),
        vmem((4, 256, 256), bf16),
        vmem((4, 256, 256), bf16),
        vmem((2, 256, 256), bf16),
        vmem((2, 256, 256), bf16),
        vmem((256, 256), bf16),
        vmem((512, 512), bf16),
        vmem((128, NY), bf16),
        vmem((8, NY), jnp.int32),
        vmem((COILS, 2, 256, 512), bf16),
        vmem((2, 128, 512), bf16),
        vmem((2, 256, 1024), bf16),
        vmem((2, 2, 256, 512), bf16),
        vmem((2, 2, 256, 512), bf16),
        vmem((2, 256, 1024), bf16),
        vmem((2, 256, 1024)),
        vmem((NZ, 2 * NY)),
        vmem((NZ + 8, 2 * NY)),
        vmem((NZ, 2 * NY)),
        vmem((NZ, 2 * NY)),
        vmem((NZ, 2 * NY)),
        vmem((NZ + 8, 2 * NY)),
        vmem((NZ, 2 * NY)),
        vmem((2, NZ, 2 * NY)),
        vmem((2, NZ, 2 * NY)),
        vmem((JOBS, ROWS, NY)),
        vmem((JOBS, HALF, NY)),
        vmem((JOBS, HALF, NY)),
        vmem((3, JOBS, HALF, NY)),
        vmem((JOBS, ROWS, NY)),
        vmem((3, 8, 128)),
        vmem((19, 8, 128)),
        vmem((8, 128)),
        dma(10 + 2 * COILS),
        dma(JOBS),
        dma(JOBS),
        dma(JOBS),
        dma(JOBS),
        dma(JOBS),
        dma(JOBS),
        dma(3, JOBS),
        dma(3, JOBS),
        dma(JOBS),
        dma(JOBS),
        dma(19),
        dma(19),
        dma(CHUNKS),
    ]
    solved = pl.pallas_call(
        kernel,
        out_shape=jax.ShapeDtypeStruct((NZ, 2 * NY), f32),
        in_specs=[anywhere] * 12,
        out_specs=anywhere,
        scratch_shapes=scratch,
        compiler_params=pltpu.CompilerParams(
            collective_id=0, has_side_effects=True, vmem_limit_bytes=60 * 2**20
        ),
        name="solve",
    )(acquired, coil_maps, words, image, *consts)
    return solved.reshape(start_image.shape)


def solution(mesh):
    in_specs = (
        P("echo", None, "plane", None, None),
        P(None, "plane", None, None),
        P("echo", None, None),
        P("echo", "plane", None, None),
    )
    out_specs = P("echo", "plane", None, None)
    return jax.shard_map(shards, mesh=mesh, in_specs=in_specs, out_specs=out_specs, check_vma=False)
```

```python
import functools
import math

import jax
import jax.numpy as jnp
import ml_dtypes
import numpy as np
from jax import lax
from jax.experimental import pallas as pl
from jax.experimental.pallas import tpu as pltpu
from jax.sharding import PartitionSpec as P

NY = 512
NZ = 256
COILS = 8
RADIUS_FACTOR = 0.5
EPSILON = 1e-06
ROWS = 32
CHUNKS = NZ // ROWS
JOBS = 2 * CHUNKS
MESH = pl.DeviceIdType.MESH
bf16 = jnp.bfloat16
f32 = jnp.float32

HALF = ROWS // 2

BEFORE = 1
AHEAD = 3
ORDER = ("pow", "us", "sh", "to", "sq", "pr", "ha", "coil", "fin")
STEPS = 53
PLANS = {
    "pow": 0x140,
    "us": 0x893,
    "to": 0x8A8B4B918400,
    "ha": 0x4A555649220,
    "sh": 0x4252697451000,
    "pr": 0x1C92934B600000,
    "sq": 0x24AAAC92888,
    "coil": 0x3FEE0013F9FE,
    "fin": 0x1FE00000000000,
}


SEGMENT = 24


def plan_word(stage, segment):
    plan = PLANS[stage]
    word = jnp.int32(0)
    for i in range(-(-STEPS // SEGMENT)):
        bits = jnp.int32((plan >> (SEGMENT * i)) & (2**SEGMENT - 1))
        word = jnp.where(segment == i, bits, word)
    return word


def tables(count):
    index = np.arange(count, dtype=np.int64)
    angle = ((index[:, None] * index[None, :]) % count).astype(np.float32) * np.float32(
        2.0 * math.pi / count
    )
    scale = np.float32(1.0 / math.sqrt(count))
    return tuple(
        (part(angle).astype(np.float32) * scale).astype(ml_dtypes.bfloat16)
        for part in (np.cos, np.sin)
    )


def constants():
    cos_y, sin_y = tables(NY)
    cos_z, sin_z = tables(NZ)
    ky_forward, ky_inverse, kz_forward, kz_inverse = [], [], [], []
    for q in range(4):
        c, s = cos_y[:128, q::4], sin_y[:128, q::4]
        ky_forward.append(np.block([[c, -s], [s, c]]))
        ky_inverse.append(np.block([[c.T, s.T], [-s.T, c.T]]))
    for p in range(2):
        c, s = cos_z[p::2, :128], sin_z[p::2, :128]
        kz_forward.append(np.block([[c, s], [-s, c]]))
        kz_inverse.append(kz_forward[-1].T)
    rows = np.zeros((NZ, NZ), np.float32)
    for r in range(NZ):
        rows[r, (r % 128) * 2 + r // 128] = 1
    lanes = np.zeros((NY, NY), np.float32)
    for k in range(NY):
        lanes[k, (k % 4) * 128 + k // 4] = 1
    lane = np.arange(NY)
    ky = 4 * (lane % 128) + lane // 128
    bits = np.zeros((8, NY), np.int32)
    bits[0] = ky % 30 % 8
    spread = np.zeros((128, NY), np.float32)
    spread[ky % 30 // 8 * 32 + ky // 30, lane] = 1
    cast = lambda a: np.ascontiguousarray(np.stack(a)).astype(ml_dtypes.bfloat16)
    return (
        cast(ky_forward),
        cast(ky_inverse),
        cast(kz_forward),
        cast(kz_inverse),
        rows.astype(ml_dtypes.bfloat16),
        lanes.astype(ml_dtypes.bfloat16),
        spread.astype(ml_dtypes.bfloat16),
        bits,
    )


def dot(a, b):
    return jnp.dot(a, b, preferred_element_type=f32)


def permute_acquired(c, acq, acqp, rows, lanes, tmp):
    for n in range(4):
        sl = slice(n * 256, (n + 1) * 256)
        tmp[:, sl] = dot(rows[...], acq[c, :, sl]).astype(bf16)
    for part in range(2):
        for n in range(2):
            v = dot(
                tmp[:, part * 512 : (part + 1) * 512], lanes[:, n * 256 : (n + 1) * 256]
            ).astype(bf16)
            out = (slice(part * 128, (part + 1) * 128), slice(n * 256, (n + 1) * 256))
            acqp[(c, 0) + out] = v[:128]
            acqp[(c, 1) + out] = v[128:]


def coil_image(c, w, maps, xs):
    for b in range(NZ // 16):
        r = slice(b * 16, b * 16 + 16)
        xr, xi = [], []
        for t in range(4):
            l = slice(t * 128, (t + 1) * 128)
            h = slice(512 + t * 128, 512 + (t + 1) * 128)
            mr, mi = maps[c, r, l].astype(f32), maps[c, r, h].astype(f32)
            wr, wi = w[r, l], w[r, h]
            xr.append(mr * wr - mi * wi)
            xi.append(mr * wi + mi * wr)
        ar, ai, br, bi = xr[0] + xr[2], xi[0] + xi[2], xr[0] - xr[2], xi[0] - xi[2]
        cr, ci, dr, di = xr[1] + xr[3], xi[1] + xi[3], xr[1] - xr[3], xi[1] - xi[3]
        outs = [(ar + cr, ai + ci), (br + di, bi - dr), (ar - cr, ai - ci), (br - di, bi + dr)]
        for q, (re, im) in enumerate(outs):
            xs[r, q * 256 : q * 256 + 128] = re.astype(bf16)
            xs[r, q * 256 + 128 : q * 256 + 256] = im.astype(bf16)


def ky_forward(xs, kf, hs):
    for q in range(4):
        h = dot(xs[:, q * 256 : (q + 1) * 256], kf[q])
        s = (h[:128] + h[128:]).astype(bf16)
        d = (h[:128] - h[128:]).astype(bf16)
        l = slice(q * 128, (q + 1) * 128)
        hs[0, 0:128, l] = s[:, :128]
        hs[0, 128:256, l] = s[:, 128:]
        hs[1, 0:128, l] = d[:, :128]
        hs[1, 128:256, l] = d[:, 128:]


def kz_residual(c, hs, tf, acqp, mask, rs):
    for p in range(2):
        for n in range(2):
            l = slice(n * 256, (n + 1) * 256)
            y = dot(tf[p], hs[p, :, l])
            m = mask[p, :, l]
            for i in range(2):
                rr = slice(i * 128, (i + 1) * 128)
                rs[p, rr, l] = (y[rr] - acqp[c, p, rr, l].astype(f32)).astype(bf16) * m


def kz_inverse(rs, ti, hp):
    for n in range(2):
        l = slice(n * 256, (n + 1) * 256)
        e, o = dot(ti[0], rs[0, :, l]), dot(ti[1], rs[1, :, l])
        for first, v in ((0, (e + o).astype(bf16)), (128, (e - o).astype(bf16))):
            for k in range(2):
                base = (2 * n + k) * 256
                ll = slice(k * 128, (k + 1) * 128)
                hp[first : first + 128, base : base + 128] = v[:128, ll]
                hp[first : first + 128, base + 128 : base + 256] = v[128:, ll]


def ky_inverse(hp, ki, zs):
    for q in range(4):
        zs[:, q * 256 : (q + 1) * 256] = dot(hp[:, q * 256 : (q + 1) * 256], ki[q])


def coil_sum(coils, zs, maps, d):
    for b in range(NZ // 16):
        r = slice(b * 16, b * 16 + 16)
        sums = [None] * 8
        for i, c in enumerate(coils):
            g = [(zs[i, r, q * 256 : q * 256 + 128], zs[i, r, q * 256 + 128 : q * 256 + 256]) for q in range(4)]
            ar, ai, br, bi = g[0][0] + g[2][0], g[0][1] + g[2][1], g[0][0] - g[2][0], g[0][1] - g[2][1]
            cr, ci, dr, di = g[1][0] + g[3][0], g[1][1] + g[3][1], g[1][0] - g[3][0], g[1][1] - g[3][1]
            z = [(ar + cr, ai + ci), (br - di, bi + dr), (ar - cr, ai - ci), (br + di, bi - dr)]
            for t in range(4):
                l = slice(t * 128, (t + 1) * 128)
                h = slice(512 + t * 128, 512 + (t + 1) * 128)
                mr, mi = maps[c, r, l].astype(f32), maps[c, r, h].astype(f32)
                zr, zi = z[t]
                re, im = mr * zr + mi * zi, mr * zi - mi * zr
                sums[t] = re if i == 0 else sums[t] + re
                sums[4 + t] = im if i == 0 else sums[4 + t] + im
        for t in range(8):
            d[r, t * 128 : (t + 1) * 128] += sums[t]


def build_mask(words, turned, spread, bits, mask):
    wide = jnp.concatenate([words[...].reshape(18, NZ), jnp.zeros((14, NZ), jnp.int32)], 0)
    turned[...] = jnp.concatenate([jnp.right_shift(wide, 8 * k) & 255 for k in range(4)], 0).T
    for p in range(2):
        byte = turned[pl.ds(p, 128, stride=2), :].astype(f32).astype(bf16)
        for n in range(2):
            l = slice(n * 256, (n + 1) * 256)
            value = dot(byte, spread[:, l]).astype(jnp.int32)
            bit = jnp.right_shift(value, jnp.broadcast_to(bits[0:1, l], (128, 256))) & 1
            mask[p, :, l] = bit.astype(f32).astype(bf16)


def kernel(
    acq_hbm, maps_hbm, words_hbm, u_hbm, kf_hbm, ki_hbm, tf_hbm, ti_hbm, rows_hbm, lanes_hbm, spread_hbm, bits_hbm,
    out_hbm,
    acq, maps, words, turned, kf, ki, tf, ti, rows, lanes, spread, bits,
    acqp, mask, xs, hs, rs, hp, zs,
    cur, extra, w, d, px, pz, py, upb, pxprev,
    n2, crecv, half, xrecv, tot, pw, pw_recv, rad,
    in_sem, up_s, up_r, px_s, px_r, cs, cr, xsend, xrecv_sem, as_, ar, ps, pr, out_sem,
):
    e = lax.axis_index("echo")
    p = lax.axis_index("plane")
    core, x = lax.rem(e, 2), e // 2
    y, z = lax.rem(p, 4), p // 4
    has_up, has_down = p < 15, p > 0
    partner = (e + 1 - 2 * core, p)
    others_x = [(lax.rem(x + k, 4) * 2 + core, p) for k in (1, 2, 3)]
    others_plane = [
        (e, lax.rem(z + b, 4) * 4 + lax.rem(y + a, 4)) for a in range(4) for b in range(4) if a or b
    ]
    up, down = (e, p + 1), (e, p - 1)

    barrier = pltpu.get_barrier_semaphore()
    greet = [partner] + others_x + others_plane
    for device in greet:
        pl.semaphore_signal(barrier, inc=1, device_id=device, device_id_type=MESH)

    @pl.when(has_up)
    def _():
        pl.semaphore_signal(barrier, inc=1, device_id=up, device_id_type=MESH)

    @pl.when(has_down)
    def _():
        pl.semaphore_signal(barrier, inc=1, device_id=down, device_id_type=MESH)

    loads = [(u_hbm, cur), (words_hbm, words), (spread_hbm, spread), (bits_hbm, bits), (rows_hbm, rows), (lanes_hbm, lanes)]
    loads += [(kf_hbm, kf), (tf_hbm, tf), (ti_hbm, ti), (ki_hbm, ki)]
    for c in range(COILS):
        loads += [(acq_hbm.at[c], acq.at[c]), (maps_hbm.at[c], maps.at[c])]
    copies = [pltpu.make_async_copy(a, b, in_sem.at[i]) for i, (a, b) in enumerate(loads)]
    for copy in copies:
        copy.start()

    px[...] = jnp.zeros_like(px)
    pz[...] = jnp.zeros_like(pz)
    py[...] = jnp.zeros_like(py)
    d[...] = jnp.zeros_like(d)
    extra[NZ : NZ + 8, :] = jnp.zeros((8, 2 * NY), f32)

    copies[0].wait()

    def power_body(b, total):
        r = pl.ds(pl.multiple_of(b * 8, 8), 8)
        v = cur[r, :]
        extra[r, :] = v
        w[r, :] = v
        s = v * v
        for k in range(8):
            total = total + s[:, k * 128 : (k + 1) * 128]
        return total

    pw[0] = lax.fori_loop(0, NZ // 8, power_body, jnp.zeros((8, 128), f32), unroll=2)
    pl.semaphore_wait(barrier, len(greet) + has_up.astype(jnp.int32) + has_down.astype(jnp.int32))

    def span(c, offset=0):
        return pl.ds(pl.multiple_of(c * ROWS + offset, 8), ROWS)

    def send_up(j, source):
        it, c = j // CHUNKS, lax.rem(j, CHUNKS)
        return pltpu.make_async_remote_copy(
            src_ref=source.at[span(c)],
            dst_ref=upb.at[it, span(c)],
            send_sem=up_s.at[j],
            recv_sem=up_r.at[j],
            device_id=down,
            device_id_type=MESH,
        )

    def send_dual(j):
        it, c = j // CHUNKS, lax.rem(j, CHUNKS)
        return pltpu.make_async_remote_copy(
            src_ref=px.at[span(c)],
            dst_ref=pxprev.at[it, span(c)],
            send_sem=px_s.at[j],
            recv_sem=px_r.at[j],
            device_id=up,
            device_id_type=MESH,
        )

    mine = pl.ds(pl.multiple_of(core * HALF, 8), HALF)
    theirs = pl.ds(pl.multiple_of(HALF - core * HALF, 8), HALF)

    def send_half(j):
        return pltpu.make_async_remote_copy(
            src_ref=n2.at[j, theirs],
            dst_ref=crecv.at[j],
            send_sem=cs.at[j],
            recv_sem=cr.at[j],
            device_id=partner,
            device_id_type=MESH,
        )

    def send_x(j, k):
        return pltpu.make_async_remote_copy(
            src_ref=half.at[j],
            dst_ref=xrecv.at[k, j],
            send_sem=xsend.at[k, j],
            recv_sem=xrecv_sem.at[k, j],
            device_id=others_x[k],
            device_id_type=MESH,
        )

    def send_total(j):
        return pltpu.make_async_remote_copy(
            src_ref=tot.at[j, mine],
            dst_ref=tot.at[j, mine],
            send_sem=as_.at[j],
            recv_sem=ar.at[j],
            device_id=partner,
            device_id_type=MESH,
        )

    power_groups = [others_plane, others_x, [partner]]
    power_first = [0, 15, 18]

    def send_power(stage, k):
        slot = power_first[stage] + k
        return pltpu.make_async_remote_copy(
            src_ref=pw.at[stage],
            dst_ref=pw_recv.at[slot],
            send_sem=ps.at[slot],
            recv_sem=pr.at[slot],
            device_id=power_groups[stage][k],
            device_id_type=MESH,
        )

    for k in range(15):
        send_power(0, k).start()
    @pl.when(has_down)
    def _():
        for j in range(BEFORE):
            send_up(j, cur).start()

    for copy in copies[1:10]:
        copy.wait()
    build_mask(words, turned, spread, bits, mask)

    lane = lax.broadcasted_iota(jnp.int32, (ROWS, 2 * NY), 1) & (NY - 1)
    row = lax.broadcasted_iota(jnp.int32, (ROWS, 2 * NY), 0)

    def squares(j):
        it, c = j // CHUNKS, lax.rem(j, CHUNKS)

        @pl.when(has_up)
        def _():
            send_up(j, extra).wait_recv()

            @pl.when(it == 1)
            def _():
                send_dual(j - CHUNKS).wait_send()

        r = span(c)
        wide = extra[pl.ds(pl.multiple_of(c * ROWS, 8), ROWS + 8), :]
        here = wide[:ROWS]
        gx = jnp.where(has_up, upb[it, r, :] - here, 0.0)
        gz = jnp.where(row + c * ROWS < NZ - 1, wide[1 : ROWS + 1] - here, 0.0)
        gy = jnp.where(lane < NY - 1, pltpu.roll(here, 2 * NY - 1, 1) - here, 0.0)
        rz = span(c, 8)
        vx = px[r, :] + 0.25 * gx
        vz = pz[rz, :] + 0.25 * gz
        vy = py[r, :] + 0.25 * gy
        px[r, :] = vx
        pz[rz, :] = vz
        py[r, :] = vy
        s = vx * vx + vz * vz + vy * vy
        n2[j] = s[:, :NY] + s[:, NY:]
        send_half(j).start()

    def halves(j):
        send_half(j).wait_recv()
        half[j] = n2[j, mine, :] + crecv[j]
        for k in range(3):
            send_x(j, k).start()

    def totals(j):
        for k in range(3):
            send_x(j, k).wait_recv()
        tot[j, mine, :] = (half[j] + xrecv[0, j]) + (xrecv[1, j] + xrecv[2, j])
        send_total(j).start()

    def shrink(j):
        c = lax.rem(j, CHUNKS)
        send_total(j).wait_recv()
        s = jnp.minimum(1.0, rad[0:1, 0:1] * lax.rsqrt(tot[j]))
        s = jnp.concatenate([s, s], 1)
        r, rz = span(c), span(c, 8)
        px[r, :] = px[r, :] * s
        pz[rz, :] = pz[rz, :] * s
        py[r, :] = py[r, :] * s

        @pl.when(has_up)
        def _():
            send_dual(j).start()

    def primal(j):
        it, c = j // CHUNKS, lax.rem(j, CHUNKS)

        @pl.when(has_down)
        def _():
            send_dual(j).wait_recv()

        send_half(j).wait_send()
        for k in range(3):
            send_x(j, k).wait_send()
        send_total(j).wait_send()

        @pl.when(has_down)
        def _():
            send_up(j, cur).wait_send()

        r = span(c)
        below = jnp.where(has_down, pxprev[it, r, :], 0.0)
        wide = pz[pl.ds(pl.multiple_of(c * ROWS, 8), ROWS + 8), :]
        vy = py[r, :]
        before = jnp.where(lane > 0, pltpu.roll(vy, 1, 1), 0.0)
        g = (below - px[r, :]) + (wide[7 : ROWS + 7] - wide[8:]) + (before - vy)
        old = cur[r, :]
        new = old - 0.25 * g

        @pl.when(it == 0)
        def _():
            first = new - 0.05 * d[r, :]
            ahead = 2.0 * first - old
            cur[r, :] = first
            extra[r, :] = ahead
            w[r, :] = (0.2 / 0.36) * ahead + (0.16 / 0.36) * old
            d[r, :] = jnp.zeros((ROWS, 2 * NY), f32)

            @pl.when(has_down)
            def _():
                send_up(j + CHUNKS, extra).start()

        @pl.when(it == 1)
        def _():
            cur[r, :] = new

    def finish(c):
        r = span(c)
        cur[r, :] = cur[r, :] - 0.09 * d[r, :]
        store(c).start()

    def store(c):
        return pltpu.make_async_copy(cur.at[span(c)], out_hbm.at[span(c)], out_sem.at[c])

    def coil_permute(c):
        for i in range(2):
            at = 10 + 2 * (c + i)
            pltpu.make_async_copy(acq_hbm.at[c + i], acq.at[c + i], in_sem.at[at]).wait()
            pltpu.make_async_copy(maps_hbm.at[c + i], maps.at[c + i], in_sem.at[at + 1]).wait()
        for i in range(2):
            permute_acquired(c + i, acq, acqp, rows, lanes, xs.at[i])

    def coil_first(c):
        for i in range(2):
            coil_image(c + i, w, maps, xs.at[i])
        for i in range(2):
            ky_forward(xs.at[i], kf, hs.at[i])

    def coil_second(c):
        for i in range(2):
            kz_residual(c + i, hs.at[i], tf, acqp, mask, rs.at[i])
        for i in range(2):
            kz_inverse(rs.at[i], ti, hp.at[i])

    def coil_third(c):
        for i in range(2):
            ky_inverse(hp.at[i], ki, zs.at[i])
        coil_sum([c, c + 1], zs, maps, d)

    def power(stage_now):
        for stage in range(3):

            @pl.when(jnp.int32(stage_now) == stage)
            def _(stage=stage):
                total = pw[stage]
                for k in range(len(power_groups[stage])):
                    send_power(stage, k).wait_recv()
                    total = total + pw_recv[power_first[stage] + k]
                if stage < 2:
                    pw[stage + 1] = total
                    for k in range(len(power_groups[stage + 1])):
                        send_power(stage + 1, k).start()
                else:
                    mean = jnp.sum(total) * (1.0 / 16777216.0) + EPSILON
                    rad[...] = RADIUS_FACTOR * jnp.sqrt(jnp.broadcast_to(mean, (8, 128)))

    def start_up(j):
        @pl.when(has_down)
        def _():
            send_up(j + AHEAD, cur).start()

    def coil_work(i):
        early = i < 16
        s = i - 16
        c = 2 * jnp.where(early, i // 4, s // 3)
        part = jnp.where(early, lax.rem(i, 4), lax.rem(s, 3) + 1)
        for k, work in enumerate((coil_permute, coil_first, coil_second, coil_third)):

            @pl.when(part == k)
            def _(work=work):
                work(c)

    works = dict(
        pow=power, us=start_up, sq=squares, ha=halves, to=totals, sh=shrink, pr=primal, fin=finish, coil=coil_work
    )

    def segment(n, done):
        words = [plan_word(stage, n) for stage in ORDER]

        def step(t, done):
            after = []
            for stage, word, count in zip(ORDER, words, done):
                now = jnp.right_shift(word, t) & 1

                @pl.when(now == 1)
                def _(stage=stage, count=count):
                    works[stage](count)

                after.append(count + now)
            return tuple(after)

        return lax.fori_loop(0, SEGMENT, step, done)

    power(0)

    @pl.when(has_down)
    def _():
        for j in range(BEFORE, AHEAD):
            send_up(j, cur).start()

    done = tuple(jnp.int32(int(stage == "pow")) for stage in ORDER)
    lax.fori_loop(0, -(-STEPS // SEGMENT), segment, done)

    for stage in range(3):
        for k in range(len(power_groups[stage])):
            send_power(stage, k).wait_send()

    def drain(c, _):
        store(c).wait()

        @pl.when(has_up)
        def _():
            send_dual(c + CHUNKS).wait_send()

        return 0

    lax.fori_loop(0, CHUNKS, drain, 0)


def shards(acquired, coil_maps, mask_words, start_image):
    acquired = acquired.reshape(COILS, NZ, 2 * NY)
    coil_maps = coil_maps.reshape(COILS, NZ, 2 * NY)
    words = jnp.transpose(mask_words, (2, 0, 1))
    image = start_image.reshape(NZ, 2 * NY)
    consts = [jnp.asarray(a) for a in constants()]
    anywhere = pl.BlockSpec(memory_space=pl.ANY)
    vmem = lambda shape, dtype=f32: pltpu.VMEM(shape, dtype)
    dma = lambda *shape: pltpu.SemaphoreType.DMA(shape)
    scratch = [
        vmem((COILS, NZ, 2 * NY), bf16),
        vmem((COILS, NZ, 2 * NY), bf16),
        vmem((18, 1, NZ), jnp.int32),
        vmem((NZ, 128), jnp.int32),
        vmem((4, 256, 256), bf16),
        vmem((4, 256, 256), bf16),
        vmem((2, 256, 256), bf16),
        vmem((2, 256, 256), bf16),
        vmem((256, 256), bf16),
        vmem((512, 512), bf16),
        vmem((128, NY), bf16),
        vmem((8, NY), jnp.int32),
        vmem((COILS, 2, 256, 512), bf16),
        vmem((2, 128, 512), bf16),
        vmem((2, 256, 1024), bf16),
        vmem((2, 2, 256, 512), bf16),
        vmem((2, 2, 256, 512), bf16),
        vmem((2, 256, 1024), bf16),
        vmem((2, 256, 1024)),
        vmem((NZ, 2 * NY)),
        vmem((NZ + 8, 2 * NY)),
        vmem((NZ, 2 * NY)),
        vmem((NZ, 2 * NY)),
        vmem((NZ, 2 * NY)),
        vmem((NZ + 8, 2 * NY)),
        vmem((NZ, 2 * NY)),
        vmem((2, NZ, 2 * NY)),
        vmem((2, NZ, 2 * NY)),
        vmem((JOBS, ROWS, NY)),
        vmem((JOBS, HALF, NY)),
        vmem((JOBS, HALF, NY)),
        vmem((3, JOBS, HALF, NY)),
        vmem((JOBS, ROWS, NY)),
        vmem((3, 8, 128)),
        vmem((19, 8, 128)),
        vmem((8, 128)),
        dma(10 + 2 * COILS),
        dma(JOBS),
        dma(JOBS),
        dma(JOBS),
        dma(JOBS),
        dma(JOBS),
        dma(JOBS),
        dma(3, JOBS),
        dma(3, JOBS),
        dma(JOBS),
        dma(JOBS),
        dma(19),
        dma(19),
        dma(CHUNKS),
    ]
    solved = pl.pallas_call(
        kernel,
        out_shape=jax.ShapeDtypeStruct((NZ, 2 * NY), f32),
        in_specs=[anywhere] * 12,
        out_specs=anywhere,
        scratch_shapes=scratch,
        compiler_params=pltpu.CompilerParams(
            collective_id=0, has_side_effects=True, vmem_limit_bytes=60 * 2**20
        ),
        name="solve",
    )(acquired, coil_maps, words, image, *consts)
    return solved.reshape(start_image.shape)


def solution(mesh):
    in_specs = (
        P("echo", None, "plane", None, None),
        P(None, "plane", None, None),
        P("echo", None, None),
        P("echo", "plane", None, None),
    )
    out_specs = P("echo", "plane", None, None)
    return jax.shard_map(shards, mesh=mesh, in_specs=in_specs, out_specs=out_specs, check_vma=False)
```
